256 devices in a mesh: band: 16 (over z, y_lo), fft: 16 (over y_hi, x, core).
Axes of the slice: x: 4, y: 4 (y_hi: 2, y_lo: 2; y = y_hi * 2 + y_lo), z: 8, core: 2. Of those that a mesh axis runs over, the one named last changes fastest.
Arguments:
- wavefunctions: bfloat16 [16, 176, 30976], P('band', 'fft'), may hold values from -6 to 6
- band_occ: int32 [16], P('band'), may hold values from 0 to 2
Outputs:
- exchange_term: float32 [16, 176, 30976], P('band', 'fft')
The draws below stay inside these ranges and needn't reach their ends.
All inputs are finite; a program needn't handle non-finite values.
Results may differ from the reference program's by a relative error of at most 0.0003.
Values may be sent and summed in bfloat16 or wider, within the bound.
No kernel may reach another device: no remote copies, remote signals or barrier semaphores. Data moves between devices by JAX's collectives and lax.ppermute only.
A program may use at most 64 MiB of HBM per device.

```python
import jax
import jax.numpy as jnp
from jax import lax

NG = 176
BAND_DEV = 1
CYCLE_STEPS = 2
BANDS = 16
N_BAND = 16


def with_ends(values, rng, smallest, top_value):
    longest = values.shape.index(max(values.shape))
    spots = []
    for shift in (0, 1):
        where = [jax.random.randint(jax.random.fold_in(rng, axis), (), 0, length) for axis, length in enumerate(values.shape)]
        where[longest] = (where[longest] + shift) % values.shape[longest]
        spots.append(tuple(where))
    return values.at[spots[0]].set(smallest).at[spots[1]].set(top_value)


def steps_of(key, dims, cuts, low, largest):
    factor_of, own = 1.0, jax.random.fold_in(key, 6)
    for axis_at, blocks in cuts:
        steps = jnp.exp(jax.random.uniform(jax.random.fold_in(own, axis_at), (blocks,), jnp.float32, low / len(cuts), largest / len(cuts)))
        factor_of = factor_of * jnp.repeat(steps, dims[axis_at] // blocks).reshape([-1 if axis == axis_at else 1 for axis in range(len(dims))])
    return factor_of


def bell_draw(own_key, dims, deviation, limit, cuts=(), held_as=jnp.bfloat16):
    array = jax.random.normal(own_key, dims, jnp.float32) * deviation
    if len(cuts) > 0:
        array = steps_of(own_key, dims, cuts, -0.22, 0.18) * array
    return jnp.clip(array, min=-limit, max=limit).astype(held_as)


def setup_inputs(seed: int = 0) -> dict:
    splits = jax.random.split(jax.random.key(seed), 3)
    return {
        "wavefunctions": bell_draw(splits[0], (BANDS, NG, NG * NG), 1.0, 6.0, ((0, 16), (1, 16))),
        "band_occ": with_ends(jax.random.randint(splits[1], (BANDS,), 0, 3), jax.random.fold_in(splits[1], 1), 0, 2).astype(jnp.int32),
    }


def truncated_profile(grid_size):
    indices = jnp.arange(grid_size, dtype=jnp.int32)
    folded = jnp.minimum(indices, grid_size - indices).astype(jnp.float32)
    squares = folded * folded
    summed = squares[:, None, None] + squares[None, :, None] + squares[None, None, :]
    safe_sum = jnp.maximum(summed, 1.0)
    radius = jnp.sqrt(safe_sum)
    return jnp.where(summed > 0.5, 2.0 * (1.0 - jnp.cos(jnp.pi * radius)) / (jnp.pi * jnp.pi * safe_sum), 1.0)

def pair_potential(density, kernel):
    spectrum = jnp.fft.rfftn(density, axes=(1, 2, 3))
    return jnp.fft.irfftn(spectrum * kernel, s=density.shape[1:], axes=(1, 2, 3)).astype(jnp.float32)

def reference(wavefunctions, band_occ):
    group_count = N_BAND
    fields = wavefunctions.reshape(group_count, BAND_DEV, NG, NG, NG)
    weights = band_occ.astype(jnp.float32).reshape(group_count, BAND_DEV)
    kernel = truncated_profile(NG)[:, :, :NG // 2 + 1] * (0.25 * float(NG) ** 1.5)
    collected = jnp.zeros((group_count, BAND_DEV, NG, NG, NG), jnp.float32)
    for cycle_step in range(1, CYCLE_STEPS + 1):

        def block_terms(group_id):
            source_group = (group_id - cycle_step) % group_count
            home_block = fields[group_id].astype(jnp.float32)
            visitor = fields[source_group].astype(jnp.float32)
            home_occ = weights[group_id]
            visitor_occ = weights[source_group]
            density = (home_block[:, None] * visitor[None]).reshape(BAND_DEV * BAND_DEV, NG, NG, NG)
            potential = pair_potential(density, kernel).reshape(BAND_DEV, BAND_DEV, NG, NG, NG)
            own_terms = -0.5 * lax.optimization_barrier(jnp.sum(potential * (visitor_occ[:, None, None, None] * visitor)[None], axis=1))
            return_terms = -0.5 * lax.optimization_barrier(jnp.sum(potential * (home_occ[:, None, None, None] * home_block)[:, None], axis=0))
            return (own_terms, return_terms)
        own_terms, return_terms = lax.map(block_terms, jnp.arange(group_count, dtype=jnp.int32))
        collected = collected + own_terms + jnp.roll(return_terms, -cycle_step, axis=0)
    return collected.reshape(group_count * BAND_DEV, NG, NG * NG)
```

```python
import functools

import jax
import jax.numpy as jnp
import ml_dtypes
import numpy as np
from jax import lax
from jax.experimental import pallas as pl
from jax.experimental.pallas import tpu as pltpu
from jax.sharding import PartitionSpec as P

NG = 176
FFT = 16
SLAB = 11
LANES = 128
STEPS = 11
GROUPS = 22
ROWS = 256
OCC_ROW = 248
CELLS = 121
BLOCK = 128
EXP_ROW = 121
PARTS = 3
F32 = jnp.float32
BF16 = jnp.bfloat16

WINDOWS = []
for _j in range(8):
    _first, _offset = divmod(NG * _j, LANES)
    WINDOWS.append((_first, _offset, -(-(_offset + NG) // LANES)))

LOW = list(range(8)) + list(range(168, 176))
KZ_FIRST = list(range(128))
KZ_REST = list(range(128, 176)) + LOW


def split_table(table):
    high = table.astype(ml_dtypes.bfloat16)
    low = (table - high.astype(np.float64)).astype(ml_dtypes.bfloat16)
    return np.stack([high, low])


@functools.cache
def tables():
    index = np.arange(NG)
    phase = (index[:, None] * index[None, :] % NG) * (2.0 * np.pi / NG)
    cas = np.cos(phase) + np.sin(phase)
    lanes = np.array(KZ_FIRST + KZ_REST + KZ_REST)
    z_forward = np.zeros((400, 256))
    z_forward[112 : 112 + NG] = cas[:, lanes]
    y_forward = np.zeros((FFT, 16, 256))
    planes = np.zeros((FFT, 16, 256))
    for block in range(FFT):
        own = block * SLAB + np.arange(SLAB)
        planes[block, :SLAB, :NG] = cas[own]
        for j in range(8):
            rows = 8 * np.arange(GROUPS) + j
            y_forward[block, :SLAB, 24 * j : 24 * j + GROUPS] = cas[own][:, rows]
    y_forward = y_forward.reshape(256, 256)
    x_back = planes.reshape(256, 256)
    x_forward = x_back.T[:NG]
    y_back = y_forward.T[:192]
    z_back = np.zeros((8, 320, 384))
    for j, (_, offset, _) in enumerate(WINDOWS):
        z_back[j, :128, offset : offset + NG] = cas[KZ_FIRST]
        z_back[j, 192:256, offset : offset + NG] = cas[KZ_REST]
    return {
        "zf": split_table(z_forward),
        "yf": split_table(y_forward),
        "xf": split_table(x_forward),
        "xb": split_table(x_back),
        "yb": split_table(y_back),
        "zb": split_table(z_back),
    }


def halves(value):
    high = value.astype(BF16)
    return high, (value - high.astype(F32)).astype(BF16)


def dot(a, b):
    return jnp.dot(a, b, preferred_element_type=F32)


def dot3(a, b):
    return dot(a[0], b[0]) + dot(a[0], b[1]) + dot(a[1], b[0])


def power_of_two(exponent):
    size = jnp.abs(exponent)
    negative = exponent < 0
    result = jnp.ones(exponent.shape, F32)
    for bit in range(7):
        step = 1 << bit
        factor = jnp.where(negative, F32(2.0**-step), F32(2.0**step))
        result = jnp.where((size & step) != 0, result * factor, result)
    return result


def exponent_of(largest):
    log2 = jnp.log(jnp.maximum(largest, 1e-32)) * F32(1.0 / np.log(2.0))
    return (jnp.floor(log2 + 0.001) - 14.0).astype(jnp.int32)


def coded(block, exp_row, residual_lanes=None):
    exponent = exponent_of(jnp.max(jnp.abs(block), axis=0, keepdims=True))
    scaled = block * power_of_two(-exponent)
    whole = jnp.round(scaled)
    if residual_lanes is not None:
        whole = jnp.where(residual_lanes, jnp.round((scaled - whole) * 32768.0), whole)
        exponent = jnp.where(residual_lanes[:1], exponent - 15, exponent)
    rows = lax.broadcasted_iota(jnp.int32, block.shape, 0)
    return jnp.where(rows >= exp_row, exponent, whole.astype(jnp.int32)).astype(jnp.int16)


def decoded(block, exp_row):
    numbers = block.astype(jnp.int32)
    return numbers.astype(F32) * power_of_two(numbers[exp_row : exp_row + 1])


def compact_kernel(occ_ref, psi_ref, out_ref, scratch):
    for step in range(STEPS):
        scratch[...] = jnp.full((ROWS, LANES), occ_ref[0], jnp.int32).astype(F32)
        for group in range(GROUPS):
            tile = (group * STEPS + step) * LANES
            scratch[pl.ds(group, SLAB, stride=GROUPS), :] = psi_ref[:, tile : tile + LANES].astype(F32)
        out_ref[step] = scratch[...].astype(BF16)


def density_kernel(odd_ref, u_ref, p_ref, q_ref, zf, yf, out_ref, dens, mixed, blocks):
    odd = odd_ref[0] == 1
    for step in range(STEPS):
        lanes = slice(step * LANES, (step + 1) * LANES)
        u, p, q = (ref[step].astype(F32) for ref in (u_ref, p_ref, q_ref))
        for pair, value in enumerate((jnp.where(odd, u, q) * p, u * q)):
            dens[pair, 0, :, lanes], dens[pair, 1, :, lanes] = halves(value)
    for pair in range(2):
        for j, (first, offset, count) in enumerate(WINDOWS):
            lanes = slice(first * LANES, (first + count) * LANES)
            rows = slice(112 - offset, 112 - offset + count * LANES)
            mixed[pair, j, :ROWS] = dot3(
                (dens[pair, 0, :, lanes], dens[pair, 1, :, lanes]), (zf[0, rows], zf[1, rows])
            )
    pad = jnp.zeros((64, 256), BF16)
    low_half = lax.broadcasted_iota(jnp.int32, (ROWS, LANES), 1) < 64
    for x in range(SLAB):
        fields = []
        for pair in range(2):
            plane = jnp.concatenate(
                [mixed[pair, j, GROUPS * x : GROUPS * x + 24] for j in range(8)], axis=0
            )
            plane = [jnp.concatenate([half, pad], axis=0) for half in halves(plane)]
            fields.append(dot3((yf[0], yf[1]), plane))
        rest = jnp.where(low_half, fields[0][:, LANES:], fields[1][:, LANES:])
        for part, field in enumerate((fields[0][:, :LANES], fields[1][:, :LANES], rest)):
            for dest in range(FFT):
                start = part * BLOCK + x * SLAB
                blocks[dest, start : start + 16] = field[16 * dest : 16 * dest + 16]
    lane = lax.broadcasted_iota(jnp.int32, (BLOCK, LANES), 1)
    residual = (lane % 64) >= 48
    for dest in range(FFT):
        for part in range(PARTS):
            rows = slice(part * BLOCK, (part + 1) * BLOCK)
            used = lax.broadcasted_iota(jnp.int32, (BLOCK, LANES), 0) < CELLS
            block = jnp.where(used, blocks[dest, rows], 0.0)
            out_ref[dest, rows] = coded(block, EXP_ROW, residual if part == 2 else None)


def expand(in_ref, cells):
    for source in range(FFT):
        for part in range(PARTS):
            rows = slice(part * BLOCK, (part + 1) * BLOCK)
            cells[source, rows] = decoded(in_ref[source, rows], EXP_ROW)
        cells[source, PARTS * BLOCK :] = jnp.zeros((48, LANES), F32)


def gathered(cells, start):
    parts = []
    for part in range(PARTS):
        parts.append(
            jnp.concatenate(
                [cells[s, pl.ds(part * BLOCK + start, 16, stride=SLAB), :] for s in range(FFT)],
                axis=0,
            )
        )
    return jnp.concatenate(parts, axis=1)


def filter_kernel(in_ref, w_ref, xf, xb, out_ref, cells, blocks):
    expand(in_ref, cells)
    pad = jnp.zeros((ROWS - NG, PARTS * LANES), BF16)
    for ky in range(SLAB):
        spectrum = dot3((xf[0], xf[1]), halves(gathered(cells, ky)))
        weight = w_ref[ky]
        spectrum = spectrum * jnp.concatenate([weight[:, :LANES], weight], axis=1)
        field = dot3(
            (xb[0], xb[1]), [jnp.concatenate([half, pad], axis=0) for half in halves(spectrum)]
        )
        for part in range(PARTS):
            for dest in range(FFT):
                start = part * BLOCK + ky * SLAB
                blocks[dest, start : start + 16] = field[
                    16 * dest : 16 * dest + 16, part * LANES : (part + 1) * LANES
                ]
    used = lax.broadcasted_iota(jnp.int32, (BLOCK, LANES), 0) < CELLS
    for dest in range(FFT):
        for part in range(PARTS):
            rows = slice(part * BLOCK, (part + 1) * BLOCK)
            out_ref[dest, rows] = coded(jnp.where(used, blocks[dest, rows], 0.0), EXP_ROW)


def product_kernel(
    odd_ref, in_ref, u_ref, p_ref, q_ref, yb, zb, own_ref, to_y, to_z, cells, mixed
):
    expand(in_ref, cells)
    for x in range(SLAB):
        plane = dot3((yb[0], yb[1]), halves(gathered(cells, x)))
        for j in range(8):
            mixed[j, GROUPS * x : GROUPS * x + 24] = plane[24 * j : 24 * j + 24]
    odd = odd_ref[0] == 1

    def occupation(ref):
        return -0.5 * ref[0, 240:256].astype(F32)[8:9]

    f_u, f_p, f_q = occupation(u_ref), occupation(p_ref), occupation(q_ref)
    f_r = jnp.where(odd, f_u, f_q)
    f_own, f_send = jnp.where(odd, f_p, 0.0), jnp.where(odd, 0.0, f_p)
    pending = [[], []]

    def finish(step, v1, v2):
        u, p, q = (ref[step].astype(F32) for ref in (u_ref, p_ref, q_ref))
        v1p = v1 * p
        own_ref[step] = f_q * (v2 * q) + f_own * v1p
        to_y[step] = coded(f_r * (v1 * jnp.where(odd, u, q)), 242)
        to_z[step] = coded(f_u * (v2 * u) + f_send * v1p, 242)

    carried = {}
    used = lax.broadcasted_iota(jnp.int32, (ROWS, LANES), 0) < 242
    for j, (first, _, count) in enumerate(WINDOWS):
        rows = jnp.concatenate([mixed[j, :ROWS]], axis=0)
        rows = jnp.where(
            lax.broadcasted_iota(jnp.int32, (ROWS, PARTS * LANES), 0) < 242, rows, 0.0
        )
        high, low = halves(rows)
        width = slice(0, count * LANES)
        fields = []
        for pair in range(2):
            lhs = [
                jnp.concatenate(
                    [half[:, pair * LANES : (pair + 1) * LANES], half[:, 2 * LANES :]], axis=1
                )
                for half in (high, low)
            ]
            if pair == 0:
                rhs = [
                    jnp.concatenate([zb[h, j, 0:128, width], zb[h, j, 192:320, width]], axis=0)
                    for h in range(2)
                ]
            else:
                rhs = [zb[h, j, 0:256, width] for h in range(2)]
            fields.append(dot3(lhs, rhs))
        for k in range(count):
            step = first + k
            pieces = [field[:, k * LANES : (k + 1) * LANES] for field in fields]
            if step in carried:
                pieces = [a + b for a, b in zip(carried[step], pieces)]
            carried[step] = pieces
        limit = WINDOWS[j + 1][0] if j < 7 else STEPS
        for step in sorted(carried):
            if step < limit:
                finish(step, *carried.pop(step))


def sum_kernel(own_ref, y_ref, z_ref, out_ref, scratch):
    for step in range(STEPS):
        scratch[...] = own_ref[step] + decoded(y_ref[step], 242) + decoded(z_ref[step], 242)
        for group in range(GROUPS):
            tile = (group * STEPS + step) * LANES
            out_ref[:, tile : tile + LANES] = scratch[pl.ds(group, SLAB, stride=GROUPS), :]


VMEM = pl.BlockSpec(memory_space=pltpu.VMEM)
SMEM = pl.BlockSpec(memory_space=pltpu.SMEM)


def call(kernel, outs, in_specs, scratch, args, flops):
    shapes = [jax.ShapeDtypeStruct(*o) for o in outs]
    moved = sum(int(np.prod(a.shape)) * a.dtype.itemsize for a in list(args) + shapes)
    single = len(outs) == 1
    return pl.pallas_call(
        kernel,
        out_shape=shapes[0] if single else shapes,
        in_specs=in_specs,
        out_specs=VMEM if single else [VMEM] * len(outs),
        scratch_shapes=scratch,
        compiler_params=pltpu.CompilerParams(vmem_limit_bytes=56 * 1024 * 1024),
        cost_estimate=pl.CostEstimate(flops=flops, bytes_accessed=moved, transcendentals=0),
    )(*args)


def kernel_weights():
    def squares(indices):
        folded = jnp.minimum(indices, NG - indices).astype(F32)
        return folded * folded

    kx = squares(jnp.arange(NG, dtype=jnp.int32))
    ky = squares(lax.axis_index("fft") * SLAB + jnp.arange(SLAB, dtype=jnp.int32))
    kz = squares(jnp.asarray(KZ_FIRST + KZ_REST + KZ_REST, jnp.int32))
    summed = ky[:, None, None] + kx[None, :, None] + kz[None, None, :]
    safe = jnp.maximum(summed, 1.0)
    radius = jnp.sqrt(safe)
    profile = 2.0 * (1.0 - jnp.cos(jnp.pi * radius)) / (jnp.pi * jnp.pi * safe)
    return jnp.where(summed > 0.5, profile, 1.0) * (0.25 / float(NG) ** 1.5)


def shards(wavefunctions, band_occ):
    size = lax.axis_size("band")
    swap = [(g, g ^ 1) for g in range(size)]
    there = [(g, (g - 2 if g % 2 == 0 else g + 2) % size) for g in range(size)]
    back = [(dest, source) for source, dest in there]
    odd = (lax.axis_index("band") % 2).astype(jnp.int32).reshape(1)
    table = {name: jnp.asarray(value) for name, value in tables().items()}
    layout = (STEPS, ROWS, LANES)
    payload = ((FFT, PARTS * BLOCK, LANES), jnp.int16)
    cells = pltpu.VMEM((FFT, PARTS * BLOCK + 48, LANES), F32)
    blocks = pltpu.VMEM((FFT, PARTS * BLOCK, LANES), F32)

    u = call(
        compact_kernel, [(layout, BF16)], [SMEM, VMEM],
        [pltpu.VMEM((ROWS, LANES), F32)], (band_occ, wavefunctions[0]), 0,
    )
    q = lax.ppermute(u, "band", there)
    p = lax.ppermute(u, "band", swap)
    weights = kernel_weights()
    sent = call(
        density_kernel, [payload], [SMEM] + [VMEM] * 5,
        [
            pltpu.VMEM((2, 2, ROWS, STEPS * LANES), BF16),
            pltpu.VMEM((2, 8, ROWS + 8, 256), F32),
            blocks,
        ],
        (odd, u, p, q, table["zf"], table["yf"]), 10**9,
    )
    columns = lax.all_to_all(sent, "fft", split_axis=0, concat_axis=0, tiled=True)
    filtered = call(
        filter_kernel, [payload], [VMEM] * 4, [cells, blocks],
        (columns, weights, table["xf"], table["xb"]), 10**9,
    )
    slabs = lax.all_to_all(filtered, "fft", split_axis=0, concat_axis=0, tiled=True)
    own, to_y, to_z = call(
        product_kernel, [(layout, F32), (layout, jnp.int16), (layout, jnp.int16)],
        [SMEM] + [VMEM] * 6,
        [cells, pltpu.VMEM((8, ROWS + 8, PARTS * LANES), F32)],
        (odd, slabs, u, p, q, table["yb"], table["zb"]), 10**9,
    )
    from_z = lax.ppermute(to_z, "band", back)
    from_y = lax.ppermute(to_y, "band", swap)
    result = call(
        sum_kernel, [((SLAB, NG * NG), F32)], [VMEM] * 3,
        [pltpu.VMEM((ROWS, LANES), F32)], (own, from_y, from_z), 0,
    )
    return result[None]


def solution(mesh):
    in_specs = (P("band", "fft", None), P("band"))
    out_specs = P("band", "fft", None)
    return jax.shard_map(shards, mesh=mesh, in_specs=in_specs, out_specs=out_specs, check_vma=False)
```

```python
import functools

import jax
import jax.numpy as jnp
import ml_dtypes
import numpy as np
from jax import lax
from jax.experimental import pallas as pl
from jax.experimental.pallas import tpu as pltpu
from jax.sharding import PartitionSpec as P

NG = 176
FFT = 16
SLAB = 11
LANES = 128
STEPS = 11
GROUPS = 22
ROWS = 256
OCC_ROW = 248
CELLS = 121
BLOCK = 128
EXP_ROW = 121
PARTS = 3
F32 = jnp.float32
BF16 = jnp.bfloat16

WINDOWS = []
for _j in range(8):
    _first, _offset = divmod(NG * _j, LANES)
    WINDOWS.append((_first, _offset, -(-(_offset + NG) // LANES)))

LOW = list(range(8)) + list(range(168, 176))
KZ_FIRST = list(range(128))
KZ_REST = list(range(128, 176)) + LOW


def split_table(table):
    high = table.astype(ml_dtypes.bfloat16)
    low = (table - high.astype(np.float64)).astype(ml_dtypes.bfloat16)
    return np.stack([high, low])


@functools.cache
def tables():
    index = np.arange(NG)
    phase = (index[:, None] * index[None, :] % NG) * (2.0 * np.pi / NG)
    cas = np.cos(phase) + np.sin(phase)
    lanes = np.array(KZ_FIRST + KZ_REST + KZ_REST)
    z_forward = np.zeros((400, 256))
    z_forward[112 : 112 + NG] = cas[:, lanes]
    y_forward = np.zeros((FFT, 16, 256))
    planes = np.zeros((FFT, 16, 256))
    for block in range(FFT):
        own = block * SLAB + np.arange(SLAB)
        planes[block, :SLAB, :NG] = cas[own]
        for j in range(8):
            rows = 8 * np.arange(GROUPS) + j
            y_forward[block, :SLAB, 24 * j : 24 * j + GROUPS] = cas[own][:, rows]
    y_forward = y_forward.reshape(256, 256)
    x_back = planes.reshape(256, 256)
    x_forward = x_back.T[:NG]
    y_back = y_forward.T[:192]
    z_back = np.zeros((8, 320, 384))
    for j, (_, offset, _) in enumerate(WINDOWS):
        z_back[j, :128, offset : offset + NG] = cas[KZ_FIRST]
        z_back[j, 192:256, offset : offset + NG] = cas[KZ_REST]
    return {
        "zf": split_table(z_forward),
        "yf": split_table(y_forward),
        "xf": split_table(x_forward),
        "xb": split_table(x_back),
        "yb": split_table(y_back),
        "zb": split_table(z_back),
    }


def halves(value):
    high = value.astype(BF16)
    return high, (value - high.astype(F32)).astype(BF16)


def dot(a, b):
    return jnp.dot(a, b, preferred_element_type=F32)


def dot3(a, b):
    return dot(a[0], b[0]) + dot(a[0], b[1]) + dot(a[1], b[0])


def power_of_two(exponent):
    size = jnp.abs(exponent)
    negative = exponent < 0
    result = jnp.ones(exponent.shape, F32)
    for bit in range(7):
        step = 1 << bit
        factor = jnp.where(negative, F32(2.0**-step), F32(2.0**step))
        result = jnp.where((size & step) != 0, result * factor, result)
    return result


def exponent_of(largest):
    log2 = jnp.log(jnp.maximum(largest, 1e-32)) * F32(1.0 / np.log(2.0))
    return (jnp.floor(log2 + 0.001) - 14.0).astype(jnp.int32)


def coded(block, exp_row, residual_lanes=None):
    exponent = exponent_of(jnp.max(jnp.abs(block), axis=0, keepdims=True))
    scaled = block * power_of_two(-exponent)
    whole = jnp.round(scaled)
    if residual_lanes is not None:
        whole = jnp.where(residual_lanes, jnp.round((scaled - whole) * 32768.0), whole)
        exponent = jnp.where(residual_lanes[:1], exponent - 15, exponent)
    rows = lax.broadcasted_iota(jnp.int32, block.shape, 0)
    return jnp.where(rows >= exp_row, exponent, whole.astype(jnp.int32)).astype(jnp.int16)


def decoded(block, exp_row):
    numbers = block.astype(jnp.int32)
    return numbers.astype(F32) * power_of_two(numbers[exp_row : exp_row + 1])


def compact_kernel(occ_ref, psi_ref, out_ref, scratch):
    for step in range(STEPS):
        scratch[...] = jnp.full((ROWS, LANES), occ_ref[0], jnp.int32).astype(F32)
        for group in range(GROUPS):
            tile = (group * STEPS + step) * LANES
            scratch[pl.ds(group, SLAB, stride=GROUPS), :] = psi_ref[:, tile : tile + LANES].astype(F32)
        out_ref[step] = scratch[...].astype(BF16)


def density_kernel(
    odd_ref, u_ref, p_ref, q_ref, zf, yf_ref, out_ref, dens, mixed, blocks, yf, sem
):
    copy = pltpu.make_async_copy(yf_ref, yf, sem)
    copy.start()
    odd = odd_ref[0] == 1
    for step in range(STEPS):
        lanes = slice(step * LANES, (step + 1) * LANES)
        u, p, q = (ref[step].astype(F32) for ref in (u_ref, p_ref, q_ref))
        for pair, value in enumerate((jnp.where(odd, u, q) * p, u * q)):
            dens[pair, 0, :, lanes], dens[pair, 1, :, lanes] = halves(value)
    for pair in range(2):
        for j, (first, offset, count) in enumerate(WINDOWS):
            lanes = slice(first * LANES, (first + count) * LANES)
            rows = slice(112 - offset, 112 - offset + count * LANES)
            mixed[pair, j, :ROWS] = dot3(
                (dens[pair, 0, :, lanes], dens[pair, 1, :, lanes]), (zf[0, rows], zf[1, rows])
            )
    copy.wait()
    pad = jnp.zeros((64, 256), BF16)
    low_half = lax.broadcasted_iota(jnp.int32, (ROWS, LANES), 1) < 64
    for x in range(SLAB):
        fields = []
        for pair in range(2):
            plane = jnp.concatenate(
                [mixed[pair, j, GROUPS * x : GROUPS * x + 24] for j in range(8)], axis=0
            )
            plane = [jnp.concatenate([half, pad], axis=0) for half in halves(plane)]
            fields.append(dot3((yf[0], yf[1]), plane))
        rest = jnp.where(low_half, fields[0][:, LANES:], fields[1][:, LANES:])
        for part, field in enumerate((fields[0][:, :LANES], fields[1][:, :LANES], rest)):
            for dest in range(FFT):
                start = part * BLOCK + x * SLAB
                blocks[dest, start : start + 16] = field[16 * dest : 16 * dest + 16]
    lane = lax.broadcasted_iota(jnp.int32, (BLOCK, LANES), 1)
    residual = (lane % 64) >= 48
    for dest in range(FFT):
        for part in range(PARTS):
            rows = slice(part * BLOCK, (part + 1) * BLOCK)
            used = lax.broadcasted_iota(jnp.int32, (BLOCK, LANES), 0) < CELLS
            block = jnp.where(used, blocks[dest, rows], 0.0)
            out_ref[dest, rows] = coded(block, EXP_ROW, residual if part == 2 else None)


def expand(in_ref, cells):
    for source in range(FFT):
        for part in range(PARTS):
            rows = slice(part * BLOCK, (part + 1) * BLOCK)
            cells[source, rows] = decoded(in_ref[source, rows], EXP_ROW)
        cells[source, PARTS * BLOCK :] = jnp.zeros((48, LANES), F32)


def gathered(cells, start):
    parts = []
    for part in range(PARTS):
        parts.append(
            jnp.concatenate(
                [cells[s, pl.ds(part * BLOCK + start, 16, stride=SLAB), :] for s in range(FFT)],
                axis=0,
            )
        )
    return jnp.concatenate(parts, axis=1)


def filter_kernel(in_ref, w_ref, xf_ref, xb_ref, out_ref, cells, blocks, xf, xb, sems):
    copies = [
        pltpu.make_async_copy(xf_ref, xf, sems.at[0]),
        pltpu.make_async_copy(xb_ref, xb, sems.at[1]),
    ]
    for copy in copies:
        copy.start()
    expand(in_ref, cells)
    for copy in copies:
        copy.wait()
    pad = jnp.zeros((ROWS - NG, PARTS * LANES), BF16)
    for ky in range(SLAB):
        spectrum = dot3((xf[0], xf[1]), halves(gathered(cells, ky)))
        weight = w_ref[ky]
        spectrum = spectrum * jnp.concatenate([weight[:, :LANES], weight], axis=1)
        field = dot3(
            (xb[0], xb[1]), [jnp.concatenate([half, pad], axis=0) for half in halves(spectrum)]
        )
        for part in range(PARTS):
            for dest in range(FFT):
                start = part * BLOCK + ky * SLAB
                blocks[dest, start : start + 16] = field[
                    16 * dest : 16 * dest + 16, part * LANES : (part + 1) * LANES
                ]
    used = lax.broadcasted_iota(jnp.int32, (BLOCK, LANES), 0) < CELLS
    for dest in range(FFT):
        for part in range(PARTS):
            rows = slice(part * BLOCK, (part + 1) * BLOCK)
            out_ref[dest, rows] = coded(jnp.where(used, blocks[dest, rows], 0.0), EXP_ROW)


def product_kernel(
    odd_ref, in_ref, u_ref, p_ref, q_ref, yb, zb, own_ref, to_y, to_z, cells, mixed
):
    expand(in_ref, cells)
    for x in range(SLAB):
        plane = dot3((yb[0], yb[1]), halves(gathered(cells, x)))
        for j in range(8):
            mixed[j, GROUPS * x : GROUPS * x + 24] = plane[24 * j : 24 * j + 24]
    odd = odd_ref[0] == 1

    def occupation(ref):
        return -0.5 * ref[0, 240:256].astype(F32)[8:9]

    f_u, f_p, f_q = occupation(u_ref), occupation(p_ref), occupation(q_ref)
    f_r = jnp.where(odd, f_u, f_q)
    f_own, f_send = jnp.where(odd, f_p, 0.0), jnp.where(odd, 0.0, f_p)
    pending = [[], []]

    def finish(step, v1, v2):
        u, p, q = (ref[step].astype(F32) for ref in (u_ref, p_ref, q_ref))
        v1p = v1 * p
        own_ref[step] = f_q * (v2 * q) + f_own * v1p
        to_y[step] = coded(f_r * (v1 * jnp.where(odd, u, q)), 242)
        to_z[step] = coded(f_u * (v2 * u) + f_send * v1p, 242)

    carried = {}
    used = lax.broadcasted_iota(jnp.int32, (ROWS, LANES), 0) < 242
    for j, (first, _, count) in enumerate(WINDOWS):
        rows = jnp.concatenate([mixed[j, :ROWS]], axis=0)
        rows = jnp.where(
            lax.broadcasted_iota(jnp.int32, (ROWS, PARTS * LANES), 0) < 242, rows, 0.0
        )
        high, low = halves(rows)
        width = slice(0, count * LANES)
        fields = []
        for pair in range(2):
            lhs = [
                jnp.concatenate(
                    [half[:, pair * LANES : (pair + 1) * LANES], half[:, 2 * LANES :]], axis=1
                )
                for half in (high, low)
            ]
            if pair == 0:
                rhs = [
                    jnp.concatenate([zb[h, j, 0:128, width], zb[h, j, 192:320, width]], axis=0)
                    for h in range(2)
                ]
            else:
                rhs = [zb[h, j, 0:256, width] for h in range(2)]
            fields.append(dot3(lhs, rhs))
        for k in range(count):
            step = first + k
            pieces = [field[:, k * LANES : (k + 1) * LANES] for field in fields]
            if step in carried:
                pieces = [a + b for a, b in zip(carried[step], pieces)]
            carried[step] = pieces
        limit = WINDOWS[j + 1][0] if j < 7 else STEPS
        for step in sorted(carried):
            if step < limit:
                finish(step, *carried.pop(step))


def sum_kernel(own_ref, y_ref, z_ref, out_ref):
    for step in range(STEPS):
        total = own_ref[step] + decoded(y_ref[step], 242) + decoded(z_ref[step], 242)
        out_ref[pl.ds(step, 242, stride=STEPS), 0, :] = total[:242]


VMEM = pl.BlockSpec(memory_space=pltpu.VMEM)
SMEM = pl.BlockSpec(memory_space=pltpu.SMEM)
ANY = pl.BlockSpec(memory_space=pl.ANY)


def call(kernel, outs, in_specs, scratch, args, flops, vmem_mib):
    shapes = [jax.ShapeDtypeStruct(*o) for o in outs]
    moved = sum(int(np.prod(a.shape)) * a.dtype.itemsize for a in list(args) + shapes)
    single = len(outs) == 1
    return pl.pallas_call(
        kernel,
        out_shape=shapes[0] if single else shapes,
        in_specs=in_specs,
        out_specs=VMEM if single else [VMEM] * len(outs),
        scratch_shapes=scratch,
        compiler_params=pltpu.CompilerParams(vmem_limit_bytes=vmem_mib * 2**20),
        cost_estimate=pl.CostEstimate(flops=flops, bytes_accessed=moved, transcendentals=0),
    )(*args)


def kernel_weights():
    def squares(indices):
        folded = jnp.minimum(indices, NG - indices).astype(F32)
        return folded * folded

    kx = squares(jnp.arange(NG, dtype=jnp.int32))
    ky = squares(lax.axis_index("fft") * SLAB + jnp.arange(SLAB, dtype=jnp.int32))
    kz = squares(jnp.asarray(KZ_FIRST + KZ_REST + KZ_REST, jnp.int32))
    summed = ky[:, None, None] + kx[None, :, None] + kz[None, None, :]
    safe = jnp.maximum(summed, 1.0)
    radius = jnp.sqrt(safe)
    profile = 2.0 * (1.0 - jnp.cos(jnp.pi * radius)) / (jnp.pi * jnp.pi * safe)
    return jnp.where(summed > 0.5, profile, 1.0) * (0.25 / float(NG) ** 1.5)


def shards(wavefunctions, band_occ):
    size = lax.axis_size("band")
    swap = [(g, g ^ 1) for g in range(size)]
    there = [(g, (g - 2 if g % 2 == 0 else g + 2) % size) for g in range(size)]
    back = [(dest, source) for source, dest in there]
    odd = (lax.axis_index("band") % 2).astype(jnp.int32).reshape(1)
    table = {name: jnp.asarray(value) for name, value in tables().items()}
    layout = (STEPS, ROWS, LANES)
    payload = ((FFT, PARTS * BLOCK, LANES), jnp.int16)
    cells = pltpu.VMEM((FFT, PARTS * BLOCK + 48, LANES), F32)
    blocks = pltpu.VMEM((FFT, PARTS * BLOCK, LANES), F32)

    u = call(
        compact_kernel, [(layout, BF16)], [SMEM, VMEM],
        [pltpu.VMEM((ROWS, LANES), F32)], (band_occ, wavefunctions[0]), 0, 4,
    )
    q = lax.ppermute(u, "band", there)
    p = lax.ppermute(u, "band", swap)
    weights = kernel_weights()
    p, weights = lax.optimization_barrier((p, weights))
    sent = call(
        density_kernel, [payload], [SMEM] + [VMEM] * 4 + [ANY],
        [
            pltpu.VMEM((2, 2, ROWS, STEPS * LANES), BF16),
            pltpu.VMEM((2, 8, ROWS + 8, 256), F32),
            blocks,
            pltpu.VMEM((2, 256, 256), BF16),
            pltpu.SemaphoreType.DMA,
        ],
        (odd, u, p, q, table["zf"], table["yf"]), 10**9, 20,
    )
    columns = lax.all_to_all(sent, "fft", split_axis=0, concat_axis=0, tiled=True)
    filtered = call(
        filter_kernel, [payload], [VMEM] * 2 + [ANY] * 2,
        [
            cells,
            blocks,
            pltpu.VMEM((2, NG, 256), BF16),
            pltpu.VMEM((2, 256, 256), BF16),
            pltpu.SemaphoreType.DMA((2,)),
        ],
        (columns, weights, table["xf"], table["xb"]), 10**9, 18,
    )
    slabs = lax.all_to_all(filtered, "fft", split_axis=0, concat_axis=0, tiled=True)
    own, to_y, to_z = call(
        product_kernel, [(layout, F32), (layout, jnp.int16), (layout, jnp.int16)],
        [SMEM] + [VMEM] * 6,
        [cells, pltpu.VMEM((8, ROWS + 8, PARTS * LANES), F32)],
        (odd, slabs, u, p, q, table["yb"], table["zb"]), 10**9, 24,
    )
    from_z = lax.ppermute(to_z, "band", back)
    from_y = lax.ppermute(to_y, "band", swap)
    result = call(
        sum_kernel, [((SLAB * NG * NG // LANES, 1, LANES), F32)], [VMEM] * 3, [],
        (own, from_y, from_z), 0, 8,
    )
    return result.reshape(1, SLAB, NG * NG)


def solution(mesh):
    in_specs = (P("band", "fft", None), P("band"))
    out_specs = P("band", "fft", None)
    return jax.shard_map(shards, mesh=mesh, in_specs=in_specs, out_specs=out_specs, check_vma=False)
```

```python
import functools

import jax
import jax.numpy as jnp
import ml_dtypes
import numpy as np
from jax import lax
from jax.experimental import pallas as pl
from jax.experimental.pallas import tpu as pltpu
from jax.sharding import PartitionSpec as P

NG = 176
FFT = 16
SLAB = 11
LANES = 128
STEPS = 11
GROUPS = 22
ROWS = 256
USED = 242
SENT = 248
CELLS = 121
PARTS = 3
BLOCK = 368
WINDOW = 128
PLACES = tuple((part * 120, part * 2) for part in range(PARTS))
F32 = jnp.float32
BF16 = jnp.bfloat16

WINDOWS = []
for _j in range(8):
    _first, _offset = divmod(NG * _j, LANES)
    WINDOWS.append((_first, _offset, -(-(_offset + NG) // LANES)))

LOW = list(range(8)) + list(range(168, 176))
KZ_FIRST = list(range(128))
KZ_REST = list(range(128, 176)) + LOW


def split_table(table):
    high = table.astype(ml_dtypes.bfloat16)
    low = (table - high.astype(np.float64)).astype(ml_dtypes.bfloat16)
    return np.stack([high, low])


@functools.cache
def tables():
    index = np.arange(NG)
    phase = (index[:, None] * index[None, :] % NG) * (2.0 * np.pi / NG)
    cas = np.cos(phase) + np.sin(phase)
    lanes = np.array(KZ_FIRST + KZ_REST + KZ_REST)
    z_forward = np.zeros((400, 256))
    z_forward[112 : 112 + NG] = cas[:, lanes]
    y_forward = np.zeros((FFT, 16, 256))
    planes = np.zeros((FFT, 16, 256))
    for block in range(FFT):
        own = block * SLAB + np.arange(SLAB)
        planes[block, :SLAB, :NG] = cas[own]
        for j in range(8):
            rows = 8 * np.arange(GROUPS) + j
            y_forward[block, :SLAB, 24 * j : 24 * j + GROUPS] = cas[own][:, rows]
    y_forward = y_forward.reshape(256, 256)
    x_back = planes.reshape(256, 256)
    x_forward = x_back.T[:NG]
    y_back = y_forward.T[:192]
    z_back = np.zeros((8, 320, 384))
    for j, (_, offset, _) in enumerate(WINDOWS):
        z_back[j, :128, offset : offset + NG] = cas[KZ_FIRST]
        z_back[j, 192:256, offset : offset + NG] = cas[KZ_REST]
    return {
        "zf": split_table(z_forward),
        "yf": split_table(y_forward),
        "xf": split_table(x_forward),
        "xb": split_table(x_back),
        "yb": split_table(y_back),
        "zb": split_table(z_back),
    }


def halves(value):
    high = value.astype(BF16)
    return high, (value - high.astype(F32)).astype(BF16)


def dot(a, b):
    return jnp.dot(a, b, preferred_element_type=F32)


def dot3(a, b):
    return dot(a[0], b[0]) + dot(a[0], b[1]) + dot(a[1], b[0])


def power_of_two(exponent):
    size = jnp.abs(exponent)
    negative = exponent < 0
    result = jnp.ones(exponent.shape, F32)
    for bit in range(7):
        step = 1 << bit
        factor = jnp.where(negative, F32(2.0**-step), F32(2.0**step))
        result = jnp.where((size & step) != 0, result * factor, result)
    return result


def exponent_of(largest):
    log2 = jnp.log(jnp.maximum(largest, 1e-32)) * F32(1.0 / np.log(2.0))
    return (jnp.floor(log2 + 0.001) - 14.0).astype(jnp.int32)


def numbers(block, first, count, residual_lanes=None):
    rows = lax.broadcasted_iota(jnp.int32, block.shape, 0)
    block = jnp.where((rows >= first) & (rows < first + count), block, 0.0)
    exponent = exponent_of(jnp.max(jnp.abs(block), axis=0, keepdims=True))
    scaled = block * power_of_two(-exponent)
    whole = jnp.round(scaled)
    if residual_lanes is not None:
        whole = jnp.where(residual_lanes, jnp.round((scaled - whole) * 32768.0), whole)
        exponent = jnp.where(residual_lanes[:1], exponent - 15, exponent)
    return jnp.where(rows == first + count, exponent, whole.astype(jnp.int32))


def write_block(blocks, dest, out_ref, residual_lanes=None):
    codes = []
    for part, (window, first) in enumerate(PLACES):
        lanes = residual_lanes if part == 2 else None
        codes.append(numbers(blocks[dest, window : window + WINDOW], first, CELLS, lanes))
    rows = lax.broadcasted_iota(jnp.int32, (8, LANES), 0)
    pieces = [codes[0][:120]]
    for part in (1, 2):
        earlier = codes[part - 1][120:]
        pieces.append(jnp.where(rows < 2 * part, earlier, codes[part][:8]))
        pieces.append(codes[part][8:120] if part == 1 else codes[part][8:])
    out_ref[dest] = jnp.concatenate(pieces, axis=0).astype(jnp.int16)


def read_blocks(in_ref, cells):
    for source in range(FFT):
        block = in_ref[source].astype(jnp.int32)
        for part, (window, first) in enumerate(PLACES):
            code = block[window : window + WINDOW]
            scale = power_of_two(code[first + CELLS : first + CELLS + 1])
            cells[source, part * WINDOW : (part + 1) * WINDOW] = code.astype(F32) * scale
        cells[source, PARTS * WINDOW :] = jnp.zeros((56, LANES), F32)


def store_cells(blocks, dest, part, line, value):
    start = part * (CELLS + 1) + line * SLAB
    size = 16 if line < SLAB - 1 else SLAB
    blocks[dest, start : start + size] = value[:size]


def coded(block):
    return numbers(block, 0, USED)[:SENT].astype(jnp.int16)


def decoded(block):
    code = block.astype(jnp.int32)
    return code.astype(F32) * power_of_two(code[USED : USED + 1])


def compact_kernel(occ_ref, psi_ref, out_ref, scratch):
    for step in range(STEPS):
        scratch[...] = jnp.full((ROWS, LANES), occ_ref[0], jnp.int32).astype(F32)
        for group in range(GROUPS):
            tile = (group * STEPS + step) * LANES
            scratch[pl.ds(group, SLAB, stride=GROUPS), :] = psi_ref[:, tile : tile + LANES].astype(F32)
        out_ref[step] = scratch[:SENT].astype(BF16)


def density_kernel(
    odd_ref, u_ref, p_ref, q_ref, zf, yf_ref, out_ref, dens, mixed, blocks, yf, sem
):
    copy = pltpu.make_async_copy(yf_ref, yf, sem)
    copy.start()
    odd = odd_ref[0] == 1
    for step in range(STEPS):
        lanes = slice(step * LANES, (step + 1) * LANES)
        u, p, q = (ref[step].astype(F32) for ref in (u_ref, p_ref, q_ref))
        for pair, value in enumerate((jnp.where(odd, u, q) * p, u * q)):
            value = jnp.concatenate([value, jnp.zeros((ROWS - SENT, LANES), F32)], axis=0)
            dens[pair, 0, :, lanes], dens[pair, 1, :, lanes] = halves(value)
    for pair in range(2):
        for j, (first, offset, count) in enumerate(WINDOWS):
            lanes = slice(first * LANES, (first + count) * LANES)
            rows = slice(112 - offset, 112 - offset + count * LANES)
            mixed[pair, j, :ROWS] = dot3(
                (dens[pair, 0, :, lanes], dens[pair, 1, :, lanes]), (zf[0, rows], zf[1, rows])
            )
    copy.wait()
    pad = jnp.zeros((64, 256), BF16)
    low_half = lax.broadcasted_iota(jnp.int32, (ROWS, LANES), 1) < 64
    for x in range(SLAB):
        fields = []
        for pair in range(2):
            plane = jnp.concatenate(
                [mixed[pair, j, GROUPS * x : GROUPS * x + 24] for j in range(8)], axis=0
            )
            plane = [jnp.concatenate([half, pad], axis=0) for half in halves(plane)]
            fields.append(dot3((yf[0], yf[1]), plane))
        rest = jnp.where(low_half, fields[0][:, LANES:], fields[1][:, LANES:])
        for part, field in enumerate((fields[0][:, :LANES], fields[1][:, :LANES], rest)):
            for dest in range(FFT):
                store_cells(blocks, dest, part, x, field[16 * dest : 16 * dest + 16])
    residual = (lax.broadcasted_iota(jnp.int32, (WINDOW, LANES), 1) % 64) >= 48
    for dest in range(FFT):
        write_block(blocks, dest, out_ref, residual)


def gathered(cells, start):
    parts = []
    for part, (_, first) in enumerate(PLACES):
        begin = part * WINDOW + first + start
        parts.append(
            jnp.concatenate(
                [cells[s, pl.ds(begin, 16, stride=SLAB), :] for s in range(FFT)],
                axis=0,
            )
        )
    return jnp.concatenate(parts, axis=1)


def filter_kernel(in_ref, w_ref, xf_ref, xb_ref, out_ref, cells, blocks, xf, xb, sems):
    copies = [
        pltpu.make_async_copy(xf_ref, xf, sems.at[0]),
        pltpu.make_async_copy(xb_ref, xb, sems.at[1]),
    ]
    for copy in copies:
        copy.start()
    read_blocks(in_ref, cells)
    for copy in copies:
        copy.wait()
    for line in range(0, SLAB, 2):
        lines = range(line, min(line + 2, SLAB))
        columns = jnp.concatenate([gathered(cells, ky) for ky in lines], axis=1)
        spectrum = dot3((xf[0], xf[1]), halves(columns))
        weight = [w_ref[ky] for ky in lines]
        weight = [tile for w in weight for tile in (w[:, :LANES], w)]
        spectrum = spectrum * jnp.concatenate(weight, axis=1)
        pad = jnp.zeros((ROWS - NG, spectrum.shape[1]), BF16)
        field = dot3(
            (xb[0], xb[1]), [jnp.concatenate([half, pad], axis=0) for half in halves(spectrum)]
        )
        for place, ky in enumerate(lines):
            for part in range(PARTS):
                lanes = slice((place * PARTS + part) * LANES, (place * PARTS + part + 1) * LANES)
                for dest in range(FFT):
                    store_cells(blocks, dest, part, ky, field[16 * dest : 16 * dest + 16, lanes])
    for dest in range(FFT):
        write_block(blocks, dest, out_ref)


def product_kernel(
    odd_ref, in_ref, u_ref, p_ref, q_ref, yb, zb, own_ref, to_y, to_z, cells, mixed
):
    read_blocks(in_ref, cells)
    for x in range(SLAB):
        plane = dot3((yb[0], yb[1]), halves(gathered(cells, x)))
        for j in range(8):
            mixed[j, GROUPS * x : GROUPS * x + 24] = plane[24 * j : 24 * j + 24]
    odd = odd_ref[0] == 1

    def occupation(ref):
        return -0.5 * ref[0].astype(F32)[SENT - 1 : SENT]

    f_u, f_p, f_q = occupation(u_ref), occupation(p_ref), occupation(q_ref)
    f_r = jnp.where(odd, f_u, f_q)
    f_own, f_send = jnp.where(odd, f_p, 0.0), jnp.where(odd, 0.0, f_p)

    def finish(step, v1, v2):
        u, p, q = (ref[step].astype(F32) for ref in (u_ref, p_ref, q_ref))
        v1p = v1 * p
        own_ref[step] = f_q * (v2 * q) + f_own * v1p
        to_y[step] = coded(f_r * (v1 * jnp.where(odd, u, q)))
        to_z[step] = coded(f_u * (v2 * u) + f_send * v1p)

    carried = {}
    used = lax.broadcasted_iota(jnp.int32, (ROWS, PARTS * LANES), 0) < USED
    for j, (first, _, count) in enumerate(WINDOWS):
        high, low = halves(jnp.where(used, mixed[j, :ROWS], 0.0))
        width = slice(0, count * LANES)
        fields = []
        for pair in range(2):
            lhs = [
                jnp.concatenate(
                    [half[:, pair * LANES : (pair + 1) * LANES], half[:, 2 * LANES :]], axis=1
                )
                for half in (high, low)
            ]
            if pair == 0:
                rhs = [
                    jnp.concatenate([zb[h, j, 0:128, width], zb[h, j, 192:320, width]], axis=0)
                    for h in range(2)
                ]
            else:
                rhs = [zb[h, j, 0:256, width] for h in range(2)]
            fields.append(dot3(lhs, rhs))
        for k in range(count):
            step = first + k
            pieces = [field[:SENT, k * LANES : (k + 1) * LANES] for field in fields]
            if step in carried:
                pieces = [a + b for a, b in zip(carried[step], pieces)]
            carried[step] = pieces
        limit = WINDOWS[j + 1][0] if j < 7 else STEPS
        for step in sorted(carried):
            if step < limit:
                finish(step, *carried.pop(step))


def sum_kernel(own_ref, y_ref, z_ref, out_ref, total, sems):
    scales = [
        [power_of_two(ref[step].astype(jnp.int32)[USED : USED + 1]) for ref in (y_ref, z_ref)]
        for step in range(STEPS)
    ]
    copies = []
    for chunk, start in enumerate(range(0, USED, 64)):
        size = min(64, USED - start)
        for step in range(STEPS):
            value = own_ref[step, start : start + size]
            for ref, scale in zip((y_ref, z_ref), scales[step]):
                value += ref[step, start : start + 64].astype(jnp.int32).astype(F32)[:size] * scale
            total[pl.ds(start * STEPS + step, size, stride=STEPS), 0, :] = value
        rows = pl.ds(start * STEPS, size * STEPS)
        copies.append(pltpu.make_async_copy(total.at[rows], out_ref.at[rows], sems.at[chunk]))
        copies[-1].start()
    for copy in copies:
        copy.wait()


VMEM = pl.BlockSpec(memory_space=pltpu.VMEM)
SMEM = pl.BlockSpec(memory_space=pltpu.SMEM)
ANY = pl.BlockSpec(memory_space=pl.ANY)


def call(kernel, outs, in_specs, scratch, args, flops, vmem_mib, out_spec=VMEM):
    shapes = [jax.ShapeDtypeStruct(*o) for o in outs]
    moved = sum(int(np.prod(a.shape)) * a.dtype.itemsize for a in list(args) + shapes)
    single = len(outs) == 1
    return pl.pallas_call(
        kernel,
        out_shape=shapes[0] if single else shapes,
        in_specs=in_specs,
        out_specs=out_spec if single else [out_spec] * len(outs),
        scratch_shapes=scratch,
        compiler_params=pltpu.CompilerParams(vmem_limit_bytes=vmem_mib * 2**20),
        cost_estimate=pl.CostEstimate(flops=flops, bytes_accessed=moved, transcendentals=0),
    )(*args)


def kernel_weights():
    def squares(indices):
        folded = jnp.minimum(indices, NG - indices).astype(F32)
        return folded * folded

    kx = squares(jnp.arange(NG, dtype=jnp.int32))
    ky = squares(lax.axis_index("fft") * SLAB + jnp.arange(SLAB, dtype=jnp.int32))
    kz = squares(jnp.asarray(KZ_FIRST + KZ_REST + KZ_REST, jnp.int32))
    summed = ky[:, None, None] + kx[None, :, None] + kz[None, None, :]
    safe = jnp.maximum(summed, 1.0)
    radius = jnp.sqrt(safe)
    profile = 2.0 * (1.0 - jnp.cos(jnp.pi * radius)) / (jnp.pi * jnp.pi * safe)
    return jnp.where(summed > 0.5, profile, 1.0) * (0.25 / float(NG) ** 1.5)


def shards(wavefunctions, band_occ):
    size = lax.axis_size("band")
    swap = [(g, g ^ 1) for g in range(size)]
    there = [(g, (g - 2 if g % 2 == 0 else g + 2) % size) for g in range(size)]
    back = [(dest, source) for source, dest in there]
    odd = (lax.axis_index("band") % 2).astype(jnp.int32).reshape(1)
    table = {name: jnp.asarray(value) for name, value in tables().items()}
    layout = (STEPS, SENT, LANES)
    payload = ((FFT, BLOCK, LANES), jnp.int16)
    cells = pltpu.VMEM((FFT, PARTS * WINDOW + 56, LANES), F32)
    blocks = pltpu.VMEM((FFT, BLOCK, LANES), F32)

    u = call(
        compact_kernel, [(layout, BF16)], [SMEM, VMEM],
        [pltpu.VMEM((ROWS, LANES), F32)], (band_occ, wavefunctions[0]), 0, 4,
    )
    q = lax.ppermute(u, "band", there)
    p = lax.ppermute(u, "band", swap)
    weights = kernel_weights()
    p, weights = lax.optimization_barrier((p, weights))
    sent = call(
        density_kernel, [payload], [SMEM] + [VMEM] * 4 + [ANY],
        [
            pltpu.VMEM((2, 2, ROWS, STEPS * LANES), BF16),
            pltpu.VMEM((2, 8, ROWS + 8, 256), F32),
            blocks,
            pltpu.VMEM((2, 256, 256), BF16),
            pltpu.SemaphoreType.DMA,
        ],
        (odd, u, p, q, table["zf"], table["yf"]), 10**9, 20,
    )
    columns = lax.all_to_all(sent, "fft", split_axis=0, concat_axis=0, tiled=True)
    filtered = call(
        filter_kernel, [payload], [VMEM] * 2 + [ANY] * 2,
        [
            cells,
            blocks,
            pltpu.VMEM((2, NG, 256), BF16),
            pltpu.VMEM((2, 256, 256), BF16),
            pltpu.SemaphoreType.DMA((2,)),
        ],
        (columns, weights, table["xf"], table["xb"]), 10**9, 18,
    )
    slabs = lax.all_to_all(filtered, "fft", split_axis=0, concat_axis=0, tiled=True)
    own, to_y, to_z = call(
        product_kernel, [(layout, F32), (layout, jnp.int16), (layout, jnp.int16)],
        [SMEM] + [VMEM] * 6,
        [cells, pltpu.VMEM((8, ROWS + 8, PARTS * LANES), F32)],
        (odd, slabs, u, p, q, table["yb"], table["zb"]), 10**9, 24,
    )
    from_z = lax.ppermute(to_z, "band", back)
    from_y = lax.ppermute(to_y, "band", swap)
    result = call(
        sum_kernel, [((SLAB * NG * NG // LANES, 1, LANES), F32)], [VMEM] * 3,
        [pltpu.VMEM((SLAB * NG * NG // LANES, 1, LANES), F32), pltpu.SemaphoreType.DMA((4,))],
        (own, from_y, from_z), 0, 8, ANY,
    )
    return result.reshape(1, SLAB, NG * NG)


def solution(mesh):
    in_specs = (P("band", "fft", None), P("band"))
    out_specs = P("band", "fft", None)
    return jax.shard_map(shards, mesh=mesh, in_specs=in_specs, out_specs=out_specs, check_vma=False)
```

```python
import functools

import jax
import jax.numpy as jnp
import ml_dtypes
import numpy as np
from jax import lax
from jax.experimental import pallas as pl
from jax.experimental.pallas import tpu as pltpu
from jax.sharding import PartitionSpec as P

NG = 176
FFT = 16
SLAB = 11
LANES = 128
STEPS = 11
GROUPS = 22
ROWS = 256
USED = 242
SENT = 248
CELLS = 121
PARTS = 3
BLOCK = 368
WINDOW = 128
PLACES = tuple((part * 120, part * 2) for part in range(PARTS))
F32 = jnp.float32
BF16 = jnp.bfloat16

WINDOWS = []
for _j in range(8):
    _first, _offset = divmod(NG * _j, LANES)
    WINDOWS.append((_first, _offset, -(-(_offset + NG) // LANES)))

SHARED = tuple((first, offset) for first, offset, count in WINDOWS if count == 3)

LOW = list(range(8)) + list(range(168, 176))
KZ_FIRST = list(range(128))
KZ_REST = list(range(128, 176)) + LOW


def split_table(table):
    high = table.astype(ml_dtypes.bfloat16)
    low = (table - high.astype(np.float64)).astype(ml_dtypes.bfloat16)
    return np.stack([high, low])


@functools.cache
def tables():
    index = np.arange(NG)
    phase = (index[:, None] * index[None, :] % NG) * (2.0 * np.pi / NG)
    cas = np.cos(phase) + np.sin(phase)
    lanes = np.array(KZ_FIRST + KZ_REST + KZ_REST)
    z_forward = np.zeros((8, 256, 256))
    z_back = np.zeros((8, 256, 256))
    for j, (_, offset, count) in enumerate(WINDOWS):
        place = offset + np.arange(NG)
        if count == 3:
            place = np.where(place < LANES, place, np.where(place < 256, place, place - 256))
        z_forward[j, place] = cas[:, lanes]
        z_back[j, :128, place] = cas[:, KZ_FIRST]
        z_back[j, 128:192, place] = cas[:, KZ_REST]
    y_forward = np.zeros((NG, 256))
    x_back = np.zeros((NG, 256))
    x_back[:, :NG] = cas
    y_back = np.zeros((FFT, 16, 192))
    x_forward = np.zeros((FFT, 16, NG))
    for j in range(8):
        rows = 8 * np.arange(GROUPS) + j
        y_forward[:, 24 * j : 24 * j + GROUPS] = cas[:, rows]
        y_back[:, :SLAB, 24 * j : 24 * j + GROUPS] = cas[:, rows].reshape(FFT, SLAB, GROUPS)
    x_forward[:, :SLAB] = cas.reshape(FFT, SLAB, NG)
    y_back = y_back.reshape(256, 192).T
    x_forward = x_forward.reshape(256, NG).T
    return {
        "zf": split_table(z_forward),
        "yf": split_table(y_forward),
        "xf": split_table(x_forward),
        "xb": split_table(x_back),
        "yb": split_table(y_back),
        "zb": split_table(z_back),
    }


def halves(value):
    high = value.astype(BF16)
    return high, (value - high.astype(F32)).astype(BF16)


def dot(a, b):
    return jnp.dot(a, b, preferred_element_type=F32)


def dot3(a, b):
    return dot(a[0], b[0]) + dot(a[0], b[1]) + dot(a[1], b[0])


def power_of_two(exponent):
    size = jnp.abs(exponent)
    negative = exponent < 0
    result = jnp.ones(exponent.shape, F32)
    for bit in range(7):
        step = 1 << bit
        factor = jnp.where(negative, F32(2.0**-step), F32(2.0**step))
        result = jnp.where((size & step) != 0, result * factor, result)
    return result


def exponent_of(largest):
    log2 = jnp.log(jnp.maximum(largest, 1e-32)) * F32(1.0 / np.log(2.0))
    return (jnp.floor(log2 + 0.001) - 14.0).astype(jnp.int32)


def rounded(value):
    return (value + 12582912.0) - 12582912.0


def largest(*pieces):
    return functools.reduce(
        jnp.maximum, [jnp.max(jnp.abs(piece), axis=0, keepdims=True) for piece in pieces]
    )


def part_pieces(blocks, dest, part):
    window, first = PLACES[part]
    rows = lax.broadcasted_iota(jnp.int32, (8, LANES), 0)
    head = blocks[dest, window : window + 8]
    if first:
        head = jnp.where(rows >= first, head, 0.0)
    tail = jnp.where(rows <= first, blocks[dest, window + 120 : window + 128], 0.0)
    return head, blocks[dest, window + 8 : window + 120], tail


def write_blocks(blocks, out_ref, sizes, exponents, residual_lanes=None):
    for dest in range(FFT):
        for part in range(PARTS):
            row = part * FFT + dest
            sizes[row : row + 1] = largest(*part_pieces(blocks, dest, part))
    exponent = exponent_of(sizes[...])
    sizes[...] = power_of_two(-exponent)
    if residual_lanes is not None:
        rest = lax.broadcasted_iota(jnp.int32, exponent.shape, 0) >= 2 * FFT
        exponent = jnp.where(rest & residual_lanes, exponent - 15, exponent)
    exponents[...] = exponent
    rows = lax.broadcasted_iota(jnp.int32, (8, LANES), 0)
    for dest in range(FFT):
        codes = []
        for part in range(PARTS):
            row = part * FFT + dest
            pieces = []
            for piece in part_pieces(blocks, dest, part):
                scaled = piece * sizes[row : row + 1]
                whole = rounded(scaled)
                if residual_lanes is not None and part == 2:
                    rest = rounded((scaled - whole) * 32768.0)
                    whole = jnp.where(residual_lanes[:1], rest, whole)
                pieces.append(whole.astype(jnp.int32))
            first = PLACES[part][1]
            pieces[2] = jnp.where(rows == first + 1, exponents[row : row + 1], pieces[2])
            if part:
                earlier = codes.pop()
                pieces[0] = jnp.where(rows < first, earlier, pieces[0])
            codes += pieces
        out_ref[dest] = jnp.concatenate(codes, axis=0).astype(jnp.int16)


def read_blocks(in_ref, cells, sizes):
    for source in range(FFT):
        for part, (window, first) in enumerate(PLACES):
            row = part * FFT + source
            tiles = in_ref[source, window + 112 : window + 128].astype(F32)
            sizes[row : row + 1] = tiles[9 + first : 10 + first]
    sizes[...] = power_of_two(sizes[...].astype(jnp.int32))
    for source in range(FFT):
        block = in_ref[source].astype(jnp.int32)
        for part, (window, _) in enumerate(PLACES):
            row = part * FFT + source
            code = block[window : window + WINDOW].astype(F32)
            cells[source, part * WINDOW : (part + 1) * WINDOW] = code * sizes[row : row + 1]
        cells[source, PARTS * WINDOW :] = jnp.zeros((56, LANES), F32)


def store_field(blocks, lines, field):
    for place, line in enumerate(lines):
        for part in range(PARTS):
            lanes = slice((place * PARTS + part) * LANES, (place * PARTS + part + 1) * LANES)
            start = part * (CELLS + 1) + line * SLAB
            for dest in range(FFT):
                rows = slice(dest * SLAB, (dest + 1) * SLAB)
                blocks[dest, start : start + SLAB] = field[rows, lanes]


def coded(block):
    rows = lax.broadcasted_iota(jnp.int32, (8, LANES), 0)
    pieces = [block[: SENT - 8], jnp.where(rows < 2, block[SENT - 8 :], 0.0)]
    exponent = exponent_of(largest(*pieces))
    scale = power_of_two(-exponent)
    pieces = [rounded(piece * scale).astype(jnp.int32) for piece in pieces]
    pieces[1] = jnp.where(rows == 2, exponent, pieces[1])
    return jnp.concatenate(pieces, axis=0).astype(jnp.int16)


def decoded(block):
    code = block.astype(jnp.int32)
    return code.astype(F32) * power_of_two(code[USED : USED + 1])


def compact_kernel(occ_ref, psi_ref, out_ref, scratch):
    for step in range(STEPS):
        scratch[...] = jnp.full((ROWS, LANES), occ_ref[0], jnp.int32).astype(F32)
        for group in range(GROUPS):
            tile = (group * STEPS + step) * LANES
            scratch[pl.ds(group, SLAB, stride=GROUPS), :] = psi_ref[:, tile : tile + LANES].astype(F32)
        out_ref[step] = scratch[:SENT].astype(BF16)


def density_kernel(
    odd_ref, u_ref, p_ref, q_ref, zf, yf_ref, out_ref, dens, mixed, blocks, sizes, exponents, yf, sem
):
    copy = pltpu.make_async_copy(yf_ref, yf, sem)
    copy.start()
    odd = odd_ref[0] == 1
    lane = lax.broadcasted_iota(jnp.int32, (2 * SENT, LANES), 1)
    values = {}
    for step in range(STEPS):
        u, p, q = (ref[step].astype(F32) for ref in (u_ref, p_ref, q_ref))
        values[step] = jnp.concatenate([jnp.where(odd, u, q) * p, u * q], axis=0)
        tiles = {step: values[step]}
        for index, (first, offset) in enumerate(SHARED):
            if step == first + 2:
                tiles[STEPS + index] = jnp.where(lane >= offset, values[first], values[step])
        for place, value in tiles.items():
            lanes = slice(place * LANES, (place + 1) * LANES)
            dens[0, :, lanes], dens[1, :, lanes] = halves(value)
    for j, (first, offset, count) in enumerate(WINDOWS):
        places = (first, first + 1)
        if count == 3:
            places = (STEPS + SHARED.index((first, offset)), first + 1)
        lhs = [
            jnp.concatenate([dens[h, :, k * LANES : (k + 1) * LANES] for k in places], axis=1)
            for h in range(2)
        ]
        mixed[j] = dot3(lhs, (zf[0, j], zf[1, j]))
    copy.wait()
    low_half = lax.broadcasted_iota(jnp.int32, (192, LANES), 1) < 64

    def plane(x):
        fields = [
            jnp.concatenate(
                [mixed[j, start : start + 24] for j in range(8)], axis=0
            )
            for start in (GROUPS * x, SENT + GROUPS * x)
        ]
        rest = jnp.where(low_half, fields[0][:, LANES:], fields[1][:, LANES:])
        return jnp.concatenate([fields[0][:, :LANES], fields[1][:, :LANES], rest], axis=1)

    for line in range(0, SLAB, 2):
        lines = range(line, min(line + 2, SLAB))
        planes = jnp.concatenate([plane(x) for x in lines], axis=1)
        pad = jnp.zeros((ROWS - 192, planes.shape[1]), BF16)
        field = dot3(
            (yf[0], yf[1]), [jnp.concatenate([half, pad], axis=0) for half in halves(planes)]
        )
        store_field(blocks, lines, field)
    residual = (lax.broadcasted_iota(jnp.int32, sizes.shape, 1) % 64) >= 48
    write_blocks(blocks, out_ref, sizes, exponents, residual)


def gathered(cells, start):
    parts = []
    for part, (_, first) in enumerate(PLACES):
        begin = part * WINDOW + first + start
        parts.append(
            jnp.concatenate(
                [cells[s, pl.ds(begin, 16, stride=SLAB), :] for s in range(FFT)],
                axis=0,
            )
        )
    return jnp.concatenate(parts, axis=1)


def filter_kernel(
    in_ref, w_ref, xf_ref, xb_ref, out_ref, cells, blocks, sizes, exponents, xf, xb, sems
):
    copies = [
        pltpu.make_async_copy(xf_ref, xf, sems.at[0]),
        pltpu.make_async_copy(xb_ref, xb, sems.at[1]),
    ]
    for copy in copies:
        copy.start()
    read_blocks(in_ref, cells, sizes)
    for copy in copies:
        copy.wait()
    for line in range(0, SLAB, 2):
        lines = range(line, min(line + 2, SLAB))
        columns = jnp.concatenate([gathered(cells, ky) for ky in lines], axis=1)
        spectrum = dot3((xf[0], xf[1]), halves(columns))
        weight = [w_ref[ky] for ky in lines]
        weight = [tile for w in weight for tile in (w[:, :LANES], w)]
        spectrum = spectrum * jnp.concatenate(weight, axis=1)
        pad = jnp.zeros((ROWS - NG, spectrum.shape[1]), BF16)
        field = dot3(
            (xb[0], xb[1]), [jnp.concatenate([half, pad], axis=0) for half in halves(spectrum)]
        )
        store_field(blocks, lines, field)
    write_blocks(blocks, out_ref, sizes, exponents)


def product_kernel(
    odd_ref, in_ref, u_ref, p_ref, q_ref, yb, zb, own_ref, to_y, to_z, cells, mixed, sizes
):
    read_blocks(in_ref, cells, sizes)
    for line in range(0, SLAB, 2):
        lines = range(line, min(line + 2, SLAB))
        columns = jnp.concatenate([gathered(cells, x) for x in lines], axis=1)
        planes = dot3((yb[0], yb[1]), halves(columns))
        for place, x in enumerate(lines):
            lanes = slice(place * PARTS * LANES, (place + 1) * PARTS * LANES)
            for j in range(8):
                mixed[j, GROUPS * x : GROUPS * x + 24] = planes[24 * j : 24 * j + 24, lanes]
    odd = odd_ref[0] == 1

    def occupation(ref):
        return -0.5 * ref[0].astype(F32)[SENT - 1 : SENT]

    f_u, f_p, f_q = occupation(u_ref), occupation(p_ref), occupation(q_ref)
    f_r = jnp.where(odd, f_u, f_q)
    f_own, f_send = jnp.where(odd, f_p, 0.0), jnp.where(odd, 0.0, f_p)

    def finish(step, v1, v2):
        u, p, q = (ref[step].astype(F32) for ref in (u_ref, p_ref, q_ref))
        v1p = v1 * p
        own_ref[step] = f_q * (v2 * q) + f_own * v1p
        to_y[step] = coded(f_r * (v1 * jnp.where(odd, u, q)))
        to_z[step] = coded(f_u * (v2 * u) + f_send * v1p)

    carried = {}
    used = lax.broadcasted_iota(jnp.int32, (SENT, PARTS * LANES), 0) < USED
    lane = lax.broadcasted_iota(jnp.int32, (SENT, LANES), 1)
    for j, (first, offset, count) in enumerate(WINDOWS):
        rows = jnp.where(used, mixed[j, :SENT], 0.0)
        firsts, seconds, rest = (rows[:, part * LANES : (part + 1) * LANES] for part in range(PARTS))
        both = jnp.concatenate(
            [
                jnp.concatenate([firsts, rest], axis=1),
                jnp.concatenate([seconds, pltpu.roll(rest, 64, axis=1)], axis=1),
            ],
            axis=0,
        )
        field = dot3(halves(both), (zb[0, j], zb[1, j]))
        fields = [field[:SENT], field[SENT:]]
        for k in range(count):
            step = first + k
            pieces = [field[:, k % 2 * LANES : (k % 2 + 1) * LANES] for field in fields]
            if count == 3 and k != 1:
                own = lane >= offset if k == 0 else lane < offset
                pieces = [jnp.where(own, piece, 0.0) for piece in pieces]
            if step in carried:
                pieces = [a + b for a, b in zip(carried[step], pieces)]
            carried[step] = pieces
        limit = WINDOWS[j + 1][0] if j < 7 else STEPS
        for step in sorted(carried):
            if step < limit:
                finish(step, *carried.pop(step))


def sum_kernel(own_ref, y_ref, z_ref, out_ref, total, sems):
    scales = [
        [power_of_two(ref[step].astype(jnp.int32)[USED : USED + 1]) for ref in (y_ref, z_ref)]
        for step in range(STEPS)
    ]
    copies = []
    for chunk, start in enumerate(range(0, USED, 64)):
        size = min(64, USED - start)
        for step in range(STEPS):
            value = own_ref[step, start : start + size]
            for ref, scale in zip((y_ref, z_ref), scales[step]):
                value += ref[step, start : start + 64].astype(jnp.int32).astype(F32)[:size] * scale
            total[pl.ds(start * STEPS + step, size, stride=STEPS), 0, :] = value
        rows = pl.ds(start * STEPS, size * STEPS)
        copies.append(pltpu.make_async_copy(total.at[rows], out_ref.at[rows], sems.at[chunk]))
        copies[-1].start()
    for copy in copies:
        copy.wait()


VMEM = pl.BlockSpec(memory_space=pltpu.VMEM)
SMEM = pl.BlockSpec(memory_space=pltpu.SMEM)
ANY = pl.BlockSpec(memory_space=pl.ANY)


def call(kernel, outs, in_specs, scratch, args, flops, vmem_mib, out_spec=VMEM):
    shapes = [jax.ShapeDtypeStruct(*o) for o in outs]
    moved = sum(int(np.prod(a.shape)) * a.dtype.itemsize for a in list(args) + shapes)
    single = len(outs) == 1
    return pl.pallas_call(
        kernel,
        out_shape=shapes[0] if single else shapes,
        in_specs=in_specs,
        out_specs=out_spec if single else [out_spec] * len(outs),
        scratch_shapes=scratch,
        compiler_params=pltpu.CompilerParams(vmem_limit_bytes=vmem_mib * 2**20),
        cost_estimate=pl.CostEstimate(flops=flops, bytes_accessed=moved, transcendentals=0),
    )(*args)


def kernel_weights():
    def squares(indices):
        folded = jnp.minimum(indices, NG - indices).astype(F32)
        return folded * folded

    kx = squares(jnp.arange(NG, dtype=jnp.int32))
    ky = squares(lax.axis_index("fft") * SLAB + jnp.arange(SLAB, dtype=jnp.int32))
    kz = squares(jnp.asarray(KZ_FIRST + KZ_REST + KZ_REST, jnp.int32))
    summed = ky[:, None, None] + kx[None, :, None] + kz[None, None, :]
    safe = jnp.maximum(summed, 1.0)
    radius = jnp.sqrt(safe)
    profile = 2.0 * (1.0 - jnp.cos(jnp.pi * radius)) / (jnp.pi * jnp.pi * safe)
    return jnp.where(summed > 0.5, profile, 1.0) * (0.25 / float(NG) ** 1.5)


def shards(wavefunctions, band_occ):
    size = lax.axis_size("band")
    swap = [(g, g ^ 1) for g in range(size)]
    there = [(g, (g - 2 if g % 2 == 0 else g + 2) % size) for g in range(size)]
    back = [(dest, source) for source, dest in there]
    odd = (lax.axis_index("band") % 2).astype(jnp.int32).reshape(1)
    table = {name: jnp.asarray(value) for name, value in tables().items()}
    layout = (STEPS, SENT, LANES)
    payload = ((FFT, BLOCK, LANES), jnp.int16)
    cells = pltpu.VMEM((FFT, PARTS * WINDOW + 56, LANES), F32)
    blocks = pltpu.VMEM((FFT, BLOCK, LANES), F32)
    scales = [pltpu.VMEM((PARTS * FFT, LANES), dtype) for dtype in (F32, jnp.int32)]

    u = call(
        compact_kernel, [(layout, BF16)], [SMEM, VMEM],
        [pltpu.VMEM((ROWS, LANES), F32)], (band_occ, wavefunctions[0]), 0, 4,
    )
    q = lax.ppermute(u, "band", there)
    p = lax.ppermute(u, "band", swap)
    weights = kernel_weights()
    p, weights = lax.optimization_barrier((p, weights))
    sent = call(
        density_kernel, [payload], [SMEM] + [VMEM] * 4 + [ANY],
        [
            pltpu.VMEM((2, 2 * SENT, (STEPS + 2) * LANES), BF16),
            pltpu.VMEM((8, 2 * SENT, 256), F32),
            blocks,
            *scales,
            pltpu.VMEM((2, NG, 256), BF16),
            pltpu.SemaphoreType.DMA,
        ],
        (odd, u, p, q, table["zf"], table["yf"]), 10**9, 20,
    )
    columns = lax.all_to_all(sent, "fft", split_axis=0, concat_axis=0, tiled=True)
    filtered = call(
        filter_kernel, [payload], [VMEM] * 2 + [ANY] * 2,
        [
            cells,
            blocks,
            *scales,
            pltpu.VMEM((2, NG, 256), BF16),
            pltpu.VMEM((2, NG, 256), BF16),
            pltpu.SemaphoreType.DMA((2,)),
        ],
        (columns, weights, table["xf"], table["xb"]), 10**9, 18,
    )
    slabs = lax.all_to_all(filtered, "fft", split_axis=0, concat_axis=0, tiled=True)
    own, to_y, to_z = call(
        product_kernel, [(layout, F32), (layout, jnp.int16), (layout, jnp.int16)],
        [SMEM] + [VMEM] * 6,
        [cells, pltpu.VMEM((8, ROWS + 8, PARTS * LANES), F32), scales[0]],
        (odd, slabs, u, p, q, table["yb"], table["zb"]), 10**9, 24,
    )
    from_z = lax.ppermute(to_z, "band", back)
    from_y = lax.ppermute(to_y, "band", swap)
    result = call(
        sum_kernel, [((SLAB * NG * NG // LANES, 1, LANES), F32)], [VMEM] * 3,
        [pltpu.VMEM((SLAB * NG * NG // LANES, 1, LANES), F32), pltpu.SemaphoreType.DMA((4,))],
        (own, from_y, from_z), 0, 8, ANY,
    )
    return result.reshape(1, SLAB, NG * NG)


def solution(mesh):
    in_specs = (P("band", "fft", None), P("band"))
    out_specs = P("band", "fft", None)
    return jax.shard_map(shards, mesh=mesh, in_specs=in_specs, out_specs=out_specs, check_vma=False)
```

```python
import functools

import jax
import jax.numpy as jnp
import ml_dtypes
import numpy as np
from jax import lax
from jax.experimental import pallas as pl
from jax.experimental.pallas import tpu as pltpu
from jax.sharding import PartitionSpec as P

NG = 176
FFT = 16
SLAB = 11
LANES = 128
STEPS = 11
GROUPS = 22
ROWS = 256
USED = 242
SENT = 248
CELLS = 121
PARTS = 3
BLOCK = 368
WINDOW = 128
PLACES = tuple((part * 120, part * 2) for part in range(PARTS))
F32 = jnp.float32
BF16 = jnp.bfloat16

WINDOWS = []
for _j in range(8):
    _first, _offset = divmod(NG * _j, LANES)
    WINDOWS.append((_first, _offset, -(-(_offset + NG) // LANES)))

SHARED = tuple((first, offset) for first, offset, count in WINDOWS if count == 3)

LOW = list(range(8)) + list(range(168, 176))
KZ_FIRST = list(range(128))
KZ_REST = list(range(128, 176)) + LOW


def split_table(table):
    high = table.astype(ml_dtypes.bfloat16)
    low = (table - high.astype(np.float64)).astype(ml_dtypes.bfloat16)
    return np.stack([high, low])


@functools.cache
def tables():
    index = np.arange(NG)
    phase = (index[:, None] * index[None, :] % NG) * (2.0 * np.pi / NG)
    cas = np.cos(phase) + np.sin(phase)
    lanes = np.array(KZ_FIRST + KZ_REST + KZ_REST)
    z_forward = np.zeros((368, 256))
    z_forward[112 : 112 + NG] = cas[:, lanes]
    z_shared = np.zeros((len(SHARED), 256, 256))
    z_back = np.zeros((8, 256, 256))
    for j, (_first, offset, count) in enumerate(WINDOWS):
        place = offset + np.arange(NG)
        if count == 3:
            place = np.where(place < LANES, place, np.where(place < 256, place, place - 256))
            z_shared[SHARED.index((_first, offset)), place] = cas[:, lanes]
        z_back[j, :128, place] = cas[:, KZ_FIRST]
        z_back[j, 128:192, place] = cas[:, KZ_REST]
    y_forward = np.zeros((NG, 256))
    x_back = np.zeros((NG, 256))
    x_back[:, :NG] = cas
    y_back = np.zeros((FFT, 16, 192))
    x_forward = np.zeros((FFT, 16, NG))
    for j in range(8):
        rows = 8 * np.arange(GROUPS) + j
        y_forward[:, 24 * j : 24 * j + GROUPS] = cas[:, rows]
        y_back[:, :SLAB, 24 * j : 24 * j + GROUPS] = cas[:, rows].reshape(FFT, SLAB, GROUPS)
    x_forward[:, :SLAB] = cas.reshape(FFT, SLAB, NG)
    y_back = y_back.reshape(256, 192).T
    x_forward = x_forward.reshape(256, NG).T
    return {
        "zf": split_table(z_forward),
        "zs": split_table(z_shared),
        "yf": split_table(y_forward),
        "xf": split_table(x_forward),
        "xb": split_table(x_back),
        "yb": split_table(y_back),
        "zb": split_table(z_back),
    }


def halves(value):
    high = value.astype(BF16)
    return high, (value - high.astype(F32)).astype(BF16)


def dot(a, b):
    return jnp.dot(a, b, preferred_element_type=F32)


def dot3(a, b):
    return dot(a[0], b[0]) + dot(a[0], b[1]) + dot(a[1], b[0])


def power_of_two(exponent):
    size = jnp.abs(exponent)
    negative = exponent < 0
    result = jnp.ones(exponent.shape, F32)
    for bit in range(7):
        step = 1 << bit
        factor = jnp.where(negative, F32(2.0**-step), F32(2.0**step))
        result = jnp.where((size & step) != 0, result * factor, result)
    return result


def exponent_of(largest):
    log2 = jnp.log(jnp.maximum(largest, 1e-32)) * F32(1.0 / np.log(2.0))
    return (jnp.floor(log2 + 0.001) - 14.0).astype(jnp.int32)


def rounded(value):
    return (value + 12582912.0) - 12582912.0


def largest(*pieces):
    return functools.reduce(
        jnp.maximum, [jnp.max(jnp.abs(piece), axis=0, keepdims=True) for piece in pieces]
    )


def part_pieces(blocks, dest, part):
    window, first = PLACES[part]
    rows = lax.broadcasted_iota(jnp.int32, (8, LANES), 0)
    head = blocks[dest, window : window + 8]
    if first:
        head = jnp.where(rows >= first, head, 0.0)
    tail = jnp.where(rows <= first, blocks[dest, window + 120 : window + 128], 0.0)
    return head, blocks[dest, window + 8 : window + 120], tail


def write_blocks(blocks, out_ref, sizes, exponents, residual_lanes=None):
    for dest in range(FFT):
        for part in range(PARTS):
            row = part * FFT + dest
            sizes[row : row + 1] = largest(*part_pieces(blocks, dest, part))
    exponent = exponent_of(sizes[...])
    sizes[...] = power_of_two(-exponent)
    if residual_lanes is not None:
        rest = lax.broadcasted_iota(jnp.int32, exponent.shape, 0) >= 2 * FFT
        exponent = jnp.where(rest & residual_lanes, exponent - 15, exponent)
    exponents[...] = exponent
    rows = lax.broadcasted_iota(jnp.int32, (8, LANES), 0)
    for dest in range(FFT):
        codes = []
        for part in range(PARTS):
            row = part * FFT + dest
            pieces = []
            for piece in part_pieces(blocks, dest, part):
                scaled = piece * sizes[row : row + 1]
                whole = rounded(scaled)
                if residual_lanes is not None and part == 2:
                    rest = rounded((scaled - whole) * 32768.0)
                    whole = jnp.where(residual_lanes[:1], rest, whole)
                pieces.append(whole.astype(jnp.int32))
            first = PLACES[part][1]
            pieces[2] = jnp.where(rows == first + 1, exponents[row : row + 1], pieces[2])
            if part:
                earlier = codes.pop()
                pieces[0] = jnp.where(rows < first, earlier, pieces[0])
            codes += pieces
        out_ref[dest] = jnp.concatenate(codes, axis=0).astype(jnp.int16)


def read_blocks(in_ref, cells, sizes):
    for source in range(FFT):
        for part, (window, first) in enumerate(PLACES):
            row = part * FFT + source
            tiles = in_ref[source, window + 112 : window + 128].astype(F32)
            sizes[row : row + 1] = tiles[9 + first : 10 + first]
    sizes[...] = power_of_two(sizes[...].astype(jnp.int32))
    for source in range(FFT):
        block = in_ref[source].astype(jnp.int32)
        for part, (window, _) in enumerate(PLACES):
            row = part * FFT + source
            code = block[window : window + WINDOW].astype(F32)
            cells[source, part * WINDOW : (part + 1) * WINDOW] = code * sizes[row : row + 1]
        cells[source, PARTS * WINDOW :] = jnp.zeros((56, LANES), F32)


def store_field(blocks, lines, field):
    for place, line in enumerate(lines):
        for part in range(PARTS):
            lanes = slice((place * PARTS + part) * LANES, (place * PARTS + part + 1) * LANES)
            start = part * (CELLS + 1) + line * SLAB
            for dest in range(FFT):
                rows = slice(dest * SLAB, (dest + 1) * SLAB)
                blocks[dest, start : start + SLAB] = field[rows, lanes]


def coded(block):
    rows = lax.broadcasted_iota(jnp.int32, (8, LANES), 0)
    pieces = [block[: SENT - 8], jnp.where(rows < 2, block[SENT - 8 :], 0.0)]
    exponent = exponent_of(largest(*pieces))
    scale = power_of_two(-exponent)
    pieces = [rounded(piece * scale).astype(jnp.int32) for piece in pieces]
    pieces[1] = jnp.where(rows == 2, exponent, pieces[1])
    return jnp.concatenate(pieces, axis=0).astype(jnp.int16)


def decoded(block):
    code = block.astype(jnp.int32)
    return code.astype(F32) * power_of_two(code[USED : USED + 1])


def compact_kernel(occ_ref, psi_ref, out_ref, scratch):
    for step in range(STEPS):
        scratch[...] = jnp.full((ROWS, LANES), occ_ref[0], jnp.int32).astype(F32)
        for group in range(GROUPS):
            tile = (group * STEPS + step) * LANES
            scratch[pl.ds(group, SLAB, stride=GROUPS), :] = psi_ref[:, tile : tile + LANES].astype(F32)
        out_ref[step] = scratch[:SENT].astype(BF16)


def density_kernel(
    odd_ref, u_ref, p_ref, q_ref, zf, zs_ref, yf_ref,
    out_ref, dens, mixed, blocks, sizes, exponents, zs, yf, sems,
):
    copies = [
        pltpu.make_async_copy(zs_ref, zs, sems.at[0]),
        pltpu.make_async_copy(yf_ref, yf, sems.at[1]),
    ]
    for copy in copies:
        copy.start()
    odd = odd_ref[0] == 1
    lane = lax.broadcasted_iota(jnp.int32, (2 * SENT, LANES), 1)
    values = {}
    for step in range(STEPS):
        u, p, q = (ref[step].astype(F32) for ref in (u_ref, p_ref, q_ref))
        values[step] = jnp.concatenate([jnp.where(odd, u, q) * p, u * q], axis=0)
        tiles = {step: values[step]}
        for index, (first, offset) in enumerate(SHARED):
            if step == first + 2:
                tiles[STEPS + index] = jnp.where(lane >= offset, values[first], values[step])
        for place, value in tiles.items():
            lanes = slice(place * LANES, (place + 1) * LANES)
            dens[0, :, lanes], dens[1, :, lanes] = halves(value)
    for j, (first, offset, count) in enumerate(WINDOWS):
        if count == 2:
            lanes = slice(first * LANES, (first + 2) * LANES)
            rows = slice(112 - offset, 368 - offset)
            mixed[j] = dot3((dens[0, :, lanes], dens[1, :, lanes]), (zf[0, rows], zf[1, rows]))
    for copy in copies:
        copy.wait()
    for j, (first, offset, count) in enumerate(WINDOWS):
        if count == 3:
            index = SHARED.index((first, offset))
            lhs = [
                jnp.concatenate(
                    [dens[h, :, k * LANES : (k + 1) * LANES] for k in (STEPS + index, first + 1)],
                    axis=1,
                )
                for h in range(2)
            ]
            mixed[j] = dot3(lhs, (zs[0, index], zs[1, index]))
    low_half = lax.broadcasted_iota(jnp.int32, (192, LANES), 1) < 64

    def plane(x):
        fields = [
            jnp.concatenate(
                [mixed[j, start : start + 24] for j in range(8)], axis=0
            )
            for start in (GROUPS * x, SENT + GROUPS * x)
        ]
        rest = jnp.where(low_half, fields[0][:, LANES:], fields[1][:, LANES:])
        return jnp.concatenate([fields[0][:, :LANES], fields[1][:, :LANES], rest], axis=1)

    for line in range(0, SLAB, 2):
        lines = range(line, min(line + 2, SLAB))
        planes = jnp.concatenate([plane(x) for x in lines], axis=1)
        pad = jnp.zeros((ROWS - 192, planes.shape[1]), BF16)
        field = dot3(
            (yf[0], yf[1]), [jnp.concatenate([half, pad], axis=0) for half in halves(planes)]
        )
        store_field(blocks, lines, field)
    residual = (lax.broadcasted_iota(jnp.int32, sizes.shape, 1) % 64) >= 48
    write_blocks(blocks, out_ref, sizes, exponents, residual)


def gathered(cells, start):
    parts = []
    for part, (_, first) in enumerate(PLACES):
        begin = part * WINDOW + first + start
        parts.append(
            jnp.concatenate(
                [cells[s, pl.ds(begin, 16, stride=SLAB), :] for s in range(FFT)],
                axis=0,
            )
        )
    return jnp.concatenate(parts, axis=1)


def filter_kernel(
    in_ref, w_ref, xf_ref, xb_ref, out_ref, cells, blocks, sizes, exponents, xf, xb, sems
):
    copies = [
        pltpu.make_async_copy(xf_ref, xf, sems.at[0]),
        pltpu.make_async_copy(xb_ref, xb, sems.at[1]),
    ]
    for copy in copies:
        copy.start()
    read_blocks(in_ref, cells, sizes)
    for copy in copies:
        copy.wait()
    for line in range(0, SLAB, 2):
        lines = range(line, min(line + 2, SLAB))
        columns = jnp.concatenate([gathered(cells, ky) for ky in lines], axis=1)
        spectrum = dot3((xf[0], xf[1]), halves(columns))
        weight = [w_ref[ky] for ky in lines]
        weight = [tile for w in weight for tile in (w[:, :LANES], w)]
        spectrum = spectrum * jnp.concatenate(weight, axis=1)
        pad = jnp.zeros((ROWS - NG, spectrum.shape[1]), BF16)
        field = dot3(
            (xb[0], xb[1]), [jnp.concatenate([half, pad], axis=0) for half in halves(spectrum)]
        )
        store_field(blocks, lines, field)
    write_blocks(blocks, out_ref, sizes, exponents)


def product_kernel(
    odd_ref, in_ref, u_ref, p_ref, q_ref, yb, zb, own_ref, to_y, to_z, cells, mixed, sizes
):
    read_blocks(in_ref, cells, sizes)
    for line in range(0, SLAB, 2):
        lines = range(line, min(line + 2, SLAB))
        columns = jnp.concatenate([gathered(cells, x) for x in lines], axis=1)
        planes = dot3((yb[0], yb[1]), halves(columns))
        for place, x in enumerate(lines):
            lanes = slice(place * PARTS * LANES, (place + 1) * PARTS * LANES)
            for j in range(8):
                mixed[j, GROUPS * x : GROUPS * x + 24] = planes[24 * j : 24 * j + 24, lanes]
    odd = odd_ref[0] == 1

    def occupation(ref):
        return -0.5 * ref[0].astype(F32)[SENT - 1 : SENT]

    f_u, f_p, f_q = occupation(u_ref), occupation(p_ref), occupation(q_ref)
    f_r = jnp.where(odd, f_u, f_q)
    f_own, f_send = jnp.where(odd, f_p, 0.0), jnp.where(odd, 0.0, f_p)

    def finish(step, v1, v2):
        u, p, q = (ref[step].astype(F32) for ref in (u_ref, p_ref, q_ref))
        v1p = v1 * p
        own_ref[step] = f_q * (v2 * q) + f_own * v1p
        to_y[step] = coded(f_r * (v1 * jnp.where(odd, u, q)))
        to_z[step] = coded(f_u * (v2 * u) + f_send * v1p)

    carried = {}
    used = lax.broadcasted_iota(jnp.int32, (SENT, PARTS * LANES), 0) < USED
    lane = lax.broadcasted_iota(jnp.int32, (SENT, LANES), 1)
    for j, (first, offset, count) in enumerate(WINDOWS):
        rows = jnp.where(used, mixed[j, :SENT], 0.0)
        firsts, seconds, rest = (rows[:, part * LANES : (part + 1) * LANES] for part in range(PARTS))
        both = jnp.concatenate(
            [
                jnp.concatenate([firsts, rest], axis=1),
                jnp.concatenate([seconds, pltpu.roll(rest, 64, axis=1)], axis=1),
            ],
            axis=0,
        )
        field = dot3(halves(both), (zb[0, j], zb[1, j]))
        fields = [field[:SENT], field[SENT:]]
        for k in range(count):
            step = first + k
            pieces = [field[:, k % 2 * LANES : (k % 2 + 1) * LANES] for field in fields]
            if count == 3 and k != 1:
                own = lane >= offset if k == 0 else lane < offset
                pieces = [jnp.where(own, piece, 0.0) for piece in pieces]
            if step in carried:
                pieces = [a + b for a, b in zip(carried[step], pieces)]
            carried[step] = pieces
        limit = WINDOWS[j + 1][0] if j < 7 else STEPS
        for step in sorted(carried):
            if step < limit:
                finish(step, *carried.pop(step))


def sum_kernel(own_ref, y_ref, z_ref, out_ref, total, sems):
    scales = [
        [power_of_two(ref[step].astype(jnp.int32)[USED : USED + 1]) for ref in (y_ref, z_ref)]
        for step in range(STEPS)
    ]
    copies = []
    for chunk, start in enumerate(range(0, USED, 64)):
        size = min(64, USED - start)
        for step in range(STEPS):
            value = own_ref[step, start : start + size]
            for ref, scale in zip((y_ref, z_ref), scales[step]):
                value += ref[step, start : start + 64].astype(jnp.int32).astype(F32)[:size] * scale
            total[pl.ds(start * STEPS + step, size, stride=STEPS), 0, :] = value
        rows = pl.ds(start * STEPS, size * STEPS)
        copies.append(pltpu.make_async_copy(total.at[rows], out_ref.at[rows], sems.at[chunk]))
        copies[-1].start()
    for copy in copies:
        copy.wait()


VMEM = pl.BlockSpec(memory_space=pltpu.VMEM)
SMEM = pl.BlockSpec(memory_space=pltpu.SMEM)
ANY = pl.BlockSpec(memory_space=pl.ANY)


def call(kernel, outs, in_specs, scratch, args, flops, vmem_mib, out_spec=VMEM):
    shapes = [jax.ShapeDtypeStruct(*o) for o in outs]
    moved = sum(int(np.prod(a.shape)) * a.dtype.itemsize for a in list(args) + shapes)
    single = len(outs) == 1
    return pl.pallas_call(
        kernel,
        out_shape=shapes[0] if single else shapes,
        in_specs=in_specs,
        out_specs=out_spec if single else [out_spec] * len(outs),
        scratch_shapes=scratch,
        compiler_params=pltpu.CompilerParams(vmem_limit_bytes=vmem_mib * 2**20),
        cost_estimate=pl.CostEstimate(flops=flops, bytes_accessed=moved, transcendentals=0),
    )(*args)


def kernel_weights():
    def squares(indices):
        folded = jnp.minimum(indices, NG - indices).astype(F32)
        return folded * folded

    kx = squares(jnp.arange(NG, dtype=jnp.int32))
    ky = squares(lax.axis_index("fft") * SLAB + jnp.arange(SLAB, dtype=jnp.int32))
    kz = squares(jnp.asarray(KZ_FIRST + KZ_REST + KZ_REST, jnp.int32))
    summed = ky[:, None, None] + kx[None, :, None] + kz[None, None, :]
    safe = jnp.maximum(summed, 1.0)
    radius = jnp.sqrt(safe)
    profile = 2.0 * (1.0 - jnp.cos(jnp.pi * radius)) / (jnp.pi * jnp.pi * safe)
    return jnp.where(summed > 0.5, profile, 1.0) * (0.25 / float(NG) ** 1.5)


def shards(wavefunctions, band_occ):
    size = lax.axis_size("band")
    swap = [(g, g ^ 1) for g in range(size)]
    there = [(g, (g - 2 if g % 2 == 0 else g + 2) % size) for g in range(size)]
    back = [(dest, source) for source, dest in there]
    odd = (lax.axis_index("band") % 2).astype(jnp.int32).reshape(1)
    table = {name: jnp.asarray(value) for name, value in tables().items()}
    layout = (STEPS, SENT, LANES)
    payload = ((FFT, BLOCK, LANES), jnp.int16)
    cells = pltpu.VMEM((FFT, PARTS * WINDOW + 56, LANES), F32)
    blocks = pltpu.VMEM((FFT, BLOCK, LANES), F32)
    scales = [pltpu.VMEM((PARTS * FFT, LANES), dtype) for dtype in (F32, jnp.int32)]

    u = call(
        compact_kernel, [(layout, BF16)], [SMEM, VMEM],
        [pltpu.VMEM((ROWS, LANES), F32)], (band_occ, wavefunctions[0]), 0, 4,
    )
    q = lax.ppermute(u, "band", there)
    p = lax.ppermute(u, "band", swap)
    weights = kernel_weights()
    p, weights = lax.optimization_barrier((p, weights))
    sent = call(
        density_kernel, [payload], [SMEM] + [VMEM] * 4 + [ANY] * 2,
        [
            pltpu.VMEM((2, 2 * SENT, (STEPS + 2) * LANES), BF16),
            pltpu.VMEM((8, 2 * SENT, 256), F32),
            blocks,
            *scales,
            pltpu.VMEM((2, len(SHARED), 256, 256), BF16),
            pltpu.VMEM((2, NG, 256), BF16),
            pltpu.SemaphoreType.DMA((2,)),
        ],
        (odd, u, p, q, table["zf"], table["zs"], table["yf"]), 10**9, 20,
    )
    columns = lax.all_to_all(sent, "fft", split_axis=0, concat_axis=0, tiled=True)
    filtered = call(
        filter_kernel, [payload], [VMEM] * 2 + [ANY] * 2,
        [
            cells,
            blocks,
            *scales,
            pltpu.VMEM((2, NG, 256), BF16),
            pltpu.VMEM((2, NG, 256), BF16),
            pltpu.SemaphoreType.DMA((2,)),
        ],
        (columns, weights, table["xf"], table["xb"]), 10**9, 18,
    )
    slabs = lax.all_to_all(filtered, "fft", split_axis=0, concat_axis=0, tiled=True)
    own, to_y, to_z = call(
        product_kernel, [(layout, F32), (layout, jnp.int16), (layout, jnp.int16)],
        [SMEM] + [VMEM] * 6,
        [cells, pltpu.VMEM((8, ROWS + 8, PARTS * LANES), F32), scales[0]],
        (odd, slabs, u, p, q, table["yb"], table["zb"]), 10**9, 24,
    )
    from_z = lax.ppermute(to_z, "band", back)
    from_y = lax.ppermute(to_y, "band", swap)
    result = call(
        sum_kernel, [((SLAB * NG * NG // LANES, 1, LANES), F32)], [VMEM] * 3,
        [pltpu.VMEM((SLAB * NG * NG // LANES, 1, LANES), F32), pltpu.SemaphoreType.DMA((4,))],
        (own, from_y, from_z), 0, 8, ANY,
    )
    return result.reshape(1, SLAB, NG * NG)


def solution(mesh):
    in_specs = (P("band", "fft", None), P("band"))
    out_specs = P("band", "fft", None)
    return jax.shard_map(shards, mesh=mesh, in_specs=in_specs, out_specs=out_specs, check_vma=False)
```

```python
import functools

import jax
import jax.numpy as jnp
import ml_dtypes
import numpy as np
from jax import lax
from jax.experimental import pallas as pl
from jax.experimental.pallas import tpu as pltpu
from jax.sharding import PartitionSpec as P

NG = 176
FFT = 16
SLAB = 11
LANES = 128
STEPS = 11
GROUPS = 22
ROWS = 256
USED = 242
SENT = 248
CELLS = 121
PARTS = 3
BLOCK = 368
WINDOW = 128
PLACES = tuple((part * 120, part * 2) for part in range(PARTS))
F32 = jnp.float32
BF16 = jnp.bfloat16

WINDOWS = []
for _j in range(8):
    _first, _offset = divmod(NG * _j, LANES)
    WINDOWS.append((_first, _offset, -(-(_offset + NG) // LANES)))

SHARED = tuple((first, offset) for first, offset, count in WINDOWS if count == 3)

LOW = list(range(8)) + list(range(168, 176))
KZ_FIRST = list(range(128))
KZ_REST = list(range(128, 176)) + LOW


def split_table(table):
    high = table.astype(ml_dtypes.bfloat16)
    low = (table - high.astype(np.float64)).astype(ml_dtypes.bfloat16)
    return np.stack([high, low])


@functools.cache
def tables():
    index = np.arange(NG)
    phase = (index[:, None] * index[None, :] % NG) * (2.0 * np.pi / NG)
    cas = np.cos(phase) + np.sin(phase)
    lanes = np.array(KZ_FIRST + KZ_REST + KZ_REST)
    z_forward = np.zeros((368, 256))
    z_forward[112 : 112 + NG] = cas[:, lanes]
    z_shared = np.zeros((len(SHARED), 256, 256))
    z_back = np.zeros((8, 256, 256))
    for j, (_first, offset, count) in enumerate(WINDOWS):
        place = offset + np.arange(NG)
        if count == 3:
            place = np.where(place < LANES, place, np.where(place < 256, place, place - 256))
            z_shared[SHARED.index((_first, offset)), place] = cas[:, lanes]
        z_back[j, :128, place] = cas[:, KZ_FIRST]
        z_back[j, 128:192, place] = cas[:, KZ_REST]
    y_forward = np.zeros((NG, 256))
    x_back = np.zeros((NG, 256))
    x_back[:, :NG] = cas
    y_back = np.zeros((FFT, 16, 192))
    x_forward = np.zeros((FFT, 16, NG))
    for j in range(8):
        rows = 8 * np.arange(GROUPS) + j
        y_forward[:, 24 * j : 24 * j + GROUPS] = cas[:, rows]
        y_back[:, :SLAB, 24 * j : 24 * j + GROUPS] = cas[:, rows].reshape(FFT, SLAB, GROUPS)
    x_forward[:, :SLAB] = cas.reshape(FFT, SLAB, NG)
    y_back = y_back.reshape(256, 192).T
    x_forward = x_forward.reshape(256, NG).T
    return {
        "zf": split_table(z_forward),
        "zs": split_table(z_shared),
        "yf": split_table(y_forward),
        "xf": split_table(x_forward),
        "xb": split_table(x_back),
        "yb": split_table(y_back),
        "zb": split_table(z_back),
    }


def halves(value):
    high = value.astype(BF16)
    return high, (value - high.astype(F32)).astype(BF16)


def dot(a, b):
    return jnp.dot(a, b, preferred_element_type=F32)


def dot3(a, b):
    return dot(a[0], b[0]) + dot(a[0], b[1]) + dot(a[1], b[0])


def power_of_two(exponent):
    size = jnp.abs(exponent)
    negative = exponent < 0
    result = jnp.ones(exponent.shape, F32)
    for bit in range(7):
        step = 1 << bit
        factor = jnp.where(negative, F32(2.0**-step), F32(2.0**step))
        result = jnp.where((size & step) != 0, result * factor, result)
    return result


def exponent_of(largest):
    log2 = jnp.log(jnp.maximum(largest, 6.4e-30)) * F32(1.0 / np.log(2.0))
    return (jnp.floor(log2 + 0.001) - 14.0).astype(jnp.int32)


def rounded(value):
    return (value + 12582912.0) - 12582912.0


def largest(*pieces):
    return functools.reduce(
        jnp.maximum, [jnp.max(jnp.abs(piece), axis=0, keepdims=True) for piece in pieces]
    )


def part_pieces(blocks, dest, part):
    window, first = PLACES[part]
    rows = lax.broadcasted_iota(jnp.int32, (8, LANES), 0)
    head = blocks[dest, window : window + 8]
    if first:
        head = jnp.where(rows >= first, head, 0.0)
    tail = jnp.where(rows <= first, blocks[dest, window + 120 : window + 128], 0.0)
    return head, blocks[dest, window + 8 : window + 120], tail


def write_blocks(blocks, out_ref, sizes, exponents, residual_lanes=None):
    for dest in range(FFT):
        for part in range(PARTS):
            row = part * FFT + dest
            sizes[row : row + 1] = largest(*part_pieces(blocks, dest, part))
    exponent = exponent_of(sizes[...])
    sizes[...] = power_of_two(-exponent)
    if residual_lanes is not None:
        rest = lax.broadcasted_iota(jnp.int32, exponent.shape, 0) >= 2 * FFT
        exponent = jnp.where(rest & residual_lanes, exponent - 15, exponent)
    exponents[...] = exponent
    rows = lax.broadcasted_iota(jnp.int32, (8, LANES), 0)
    for dest in range(FFT):
        codes = []
        for part in range(PARTS):
            row = part * FFT + dest
            pieces = []
            for piece in part_pieces(blocks, dest, part):
                scaled = piece * sizes[row : row + 1]
                whole = rounded(scaled)
                if residual_lanes is not None and part == 2:
                    rest = rounded((scaled - whole) * 32768.0)
                    whole = jnp.where(residual_lanes[:1], rest, whole)
                pieces.append(whole.astype(jnp.int32))
            first = PLACES[part][1]
            pieces[2] = jnp.where(rows == first + 1, exponents[row : row + 1], pieces[2])
            if part:
                earlier = codes.pop()
                pieces[0] = jnp.where(rows < first, earlier, pieces[0])
            codes += pieces
        out_ref[dest] = jnp.concatenate(codes, axis=0).astype(jnp.int16)


def read_blocks(in_ref, cells, sizes):
    for source in range(FFT):
        for part, (window, first) in enumerate(PLACES):
            row = part * FFT + source
            tiles = in_ref[source, window + 112 : window + 128].astype(F32)
            sizes[row : row + 1] = tiles[9 + first : 10 + first]
    sizes[...] = power_of_two(sizes[...].astype(jnp.int32))
    for source in range(FFT):
        block = in_ref[source].astype(jnp.int32)
        for part, (window, _) in enumerate(PLACES):
            row = part * FFT + source
            code = block[window : window + WINDOW].astype(F32)
            cells[source, part * WINDOW : (part + 1) * WINDOW] = code * sizes[row : row + 1]
        cells[source, PARTS * WINDOW :] = jnp.zeros((56, LANES), F32)


def store_field(blocks, lines, field):
    for place, line in enumerate(lines):
        for part in range(PARTS):
            lanes = slice((place * PARTS + part) * LANES, (place * PARTS + part + 1) * LANES)
            start = part * (CELLS + 1) + line * SLAB
            for dest in range(FFT):
                rows = slice(dest * SLAB, (dest + 1) * SLAB)
                blocks[dest, start : start + SLAB] = field[rows, lanes]


def coded(block):
    rows = lax.broadcasted_iota(jnp.int32, (8, LANES), 0)
    pieces = [block[: SENT - 8], jnp.where(rows < 2, block[SENT - 8 :], 0.0)]
    exponent = exponent_of(largest(*pieces))
    scale = power_of_two(-exponent)
    pieces = [rounded(piece * scale).astype(jnp.int32) for piece in pieces]
    pieces[1] = jnp.where(rows == 2, exponent, pieces[1])
    return jnp.concatenate(pieces, axis=0).astype(jnp.int16)


def decoded(block):
    code = block.astype(jnp.int32)
    return code.astype(F32) * power_of_two(code[USED : USED + 1])


def compact_kernel(occ_ref, psi_ref, out_ref, scratch):
    for step in range(STEPS):
        scratch[...] = jnp.full((ROWS, LANES), occ_ref[0], jnp.int32).astype(F32)
        for group in range(GROUPS):
            tile = (group * STEPS + step) * LANES
            scratch[pl.ds(group, SLAB, stride=GROUPS), :] = psi_ref[:, tile : tile + LANES].astype(F32)
        out_ref[step] = scratch[:SENT].astype(BF16)


def density_kernel(
    odd_ref, u_ref, p_ref, q_ref, zf, zs, yf_ref,
    out_ref, dens, mixed, blocks, sizes, exponents, yf, sem,
):
    copy = pltpu.make_async_copy(yf_ref, yf, sem)
    copy.start()
    odd = odd_ref[0] == 1
    lane = lax.broadcasted_iota(jnp.int32, (2 * SENT, LANES), 1)
    values = {}
    for step in range(STEPS):
        u, p, q = (ref[step].astype(F32) for ref in (u_ref, p_ref, q_ref))
        values[step] = jnp.concatenate([jnp.where(odd, u, q) * p, u * q], axis=0)
        tiles = {step: values[step]}
        for index, (first, offset) in enumerate(SHARED):
            if step == first + 2:
                tiles[STEPS + index] = jnp.where(lane >= offset, values[first], values[step])
        for place, value in tiles.items():
            lanes = slice(place * LANES, (place + 1) * LANES)
            dens[0, :, lanes], dens[1, :, lanes] = halves(value)
    for j, (first, offset, count) in enumerate(WINDOWS):
        if count == 2:
            places = (first, first + 1)
            rows = slice(112 - offset, 368 - offset)
            table = (zf[0, rows], zf[1, rows])
        else:
            index = SHARED.index((first, offset))
            places = (STEPS + index, first + 1)
            table = (zs[0, index], zs[1, index])
        lhs = [
            jnp.concatenate([dens[h, :, k * LANES : (k + 1) * LANES] for k in places], axis=1)
            for h in range(2)
        ]
        mixed[j] = dot3(lhs, table)
    copy.wait()
    low_half = lax.broadcasted_iota(jnp.int32, (192, LANES), 1) < 64

    def plane(x):
        fields = [
            jnp.concatenate(
                [mixed[j, start : start + 24] for j in range(8)], axis=0
            )
            for start in (GROUPS * x, SENT + GROUPS * x)
        ]
        rest = jnp.where(low_half, fields[0][:, LANES:], fields[1][:, LANES:])
        return jnp.concatenate([fields[0][:, :LANES], fields[1][:, :LANES], rest], axis=1)

    for line in range(0, SLAB, 2):
        lines = range(line, min(line + 2, SLAB))
        planes = jnp.concatenate([plane(x) for x in lines], axis=1)
        pad = jnp.zeros((ROWS - 192, planes.shape[1]), BF16)
        field = dot3(
            (yf[0], yf[1]), [jnp.concatenate([half, pad], axis=0) for half in halves(planes)]
        )
        store_field(blocks, lines, field)
    residual = (lax.broadcasted_iota(jnp.int32, sizes.shape, 1) % 64) >= 48
    write_blocks(blocks, out_ref, sizes, exponents, residual)


def gathered(cells, start):
    parts = []
    for part, (_, first) in enumerate(PLACES):
        begin = part * WINDOW + first + start
        parts.append(
            jnp.concatenate(
                [cells[s, pl.ds(begin, 16, stride=SLAB), :] for s in range(FFT)],
                axis=0,
            )
        )
    return jnp.concatenate(parts, axis=1)


def filter_kernel(
    in_ref, w_ref, xf_ref, xb_ref, out_ref, cells, blocks, sizes, exponents, xf, xb, sems
):
    copies = [
        pltpu.make_async_copy(xf_ref, xf, sems.at[0]),
        pltpu.make_async_copy(xb_ref, xb, sems.at[1]),
    ]
    for copy in copies:
        copy.start()
    read_blocks(in_ref, cells, sizes)
    for copy in copies:
        copy.wait()
    for line in range(0, SLAB, 2):
        lines = range(line, min(line + 2, SLAB))
        columns = jnp.concatenate([gathered(cells, ky) for ky in lines], axis=1)
        spectrum = dot3((xf[0], xf[1]), halves(columns))
        weight = [w_ref[ky] for ky in lines]
        weight = [tile for w in weight for tile in (w[:, :LANES], w)]
        spectrum = spectrum * jnp.concatenate(weight, axis=1)
        pad = jnp.zeros((ROWS - NG, spectrum.shape[1]), BF16)
        field = dot3(
            (xb[0], xb[1]), [jnp.concatenate([half, pad], axis=0) for half in halves(spectrum)]
        )
        store_field(blocks, lines, field)
    write_blocks(blocks, out_ref, sizes, exponents)


def product_kernel(
    odd_ref, in_ref, u_ref, p_ref, q_ref, yb, zb, own_ref, to_y, to_z, cells, mixed, sizes
):
    read_blocks(in_ref, cells, sizes)
    for line in range(0, SLAB, 2):
        lines = range(line, min(line + 2, SLAB))
        columns = jnp.concatenate([gathered(cells, x) for x in lines], axis=1)
        planes = dot3((yb[0], yb[1]), halves(columns))
        for place, x in enumerate(lines):
            lanes = slice(place * PARTS * LANES, (place + 1) * PARTS * LANES)
            for j in range(8):
                mixed[j, GROUPS * x : GROUPS * x + 24] = planes[24 * j : 24 * j + 24, lanes]
    odd = odd_ref[0] == 1

    def occupation(ref):
        return -0.5 * ref[0].astype(F32)[SENT - 1 : SENT]

    f_u, f_p, f_q = occupation(u_ref), occupation(p_ref), occupation(q_ref)
    f_r = jnp.where(odd, f_u, f_q)
    f_own, f_send = jnp.where(odd, f_p, 0.0), jnp.where(odd, 0.0, f_p)

    def finish(step, v1, v2):
        u, p, q = (ref[step].astype(F32) for ref in (u_ref, p_ref, q_ref))
        v1p = v1 * p
        own_ref[step] = f_q * (v2 * q) + f_own * v1p
        to_y[step] = coded(f_r * (v1 * jnp.where(odd, u, q)))
        to_z[step] = coded(f_u * (v2 * u) + f_send * v1p)

    carried = {}
    used = lax.broadcasted_iota(jnp.int32, (SENT, PARTS * LANES), 0) < USED
    lane = lax.broadcasted_iota(jnp.int32, (SENT, LANES), 1)
    for j, (first, offset, count) in enumerate(WINDOWS):
        rows = jnp.where(used, mixed[j, :SENT], 0.0)
        firsts, seconds, rest = (rows[:, part * LANES : (part + 1) * LANES] for part in range(PARTS))
        both = jnp.concatenate(
            [
                jnp.concatenate([firsts, rest], axis=1),
                jnp.concatenate([seconds, pltpu.roll(rest, 64, axis=1)], axis=1),
            ],
            axis=0,
        )
        field = dot3(halves(both), (zb[0, j], zb[1, j]))
        fields = [field[:SENT], field[SENT:]]
        for k in range(count):
            step = first + k
            pieces = [field[:, k % 2 * LANES : (k % 2 + 1) * LANES] for field in fields]
            if count == 3 and k != 1:
                own = lane >= offset if k == 0 else lane < offset
                pieces = [jnp.where(own, piece, 0.0) for piece in pieces]
            if step in carried:
                pieces = [a + b for a, b in zip(carried[step], pieces)]
            carried[step] = pieces
        limit = WINDOWS[j + 1][0] if j < 7 else STEPS
        for step in sorted(carried):
            if step < limit:
                finish(step, *carried.pop(step))


def sum_kernel(own_ref, y_ref, z_ref, out_ref, total, sems):
    scales = [
        [power_of_two(ref[step].astype(jnp.int32)[USED : USED + 1]) for ref in (y_ref, z_ref)]
        for step in range(STEPS)
    ]
    copies = []
    for chunk, start in enumerate(range(0, USED, 64)):
        size = min(64, USED - start)
        for step in range(STEPS):
            value = own_ref[step, start : start + size]
            for ref, scale in zip((y_ref, z_ref), scales[step]):
                value += ref[step, start : start + 64].astype(jnp.int32).astype(F32)[:size] * scale
            total[pl.ds(start * STEPS + step, size, stride=STEPS), 0, :] = value
        rows = pl.ds(start * STEPS, size * STEPS)
        copies.append(pltpu.make_async_copy(total.at[rows], out_ref.at[rows], sems.at[chunk]))
        copies[-1].start()
    for copy in copies:
        copy.wait()


VMEM = pl.BlockSpec(memory_space=pltpu.VMEM)
SMEM = pl.BlockSpec(memory_space=pltpu.SMEM)
ANY = pl.BlockSpec(memory_space=pl.ANY)


def call(kernel, outs, in_specs, scratch, args, flops, vmem_mib, out_spec=VMEM):
    shapes = [jax.ShapeDtypeStruct(*o) for o in outs]
    moved = sum(int(np.prod(a.shape)) * a.dtype.itemsize for a in list(args) + shapes)
    single = len(outs) == 1
    return pl.pallas_call(
        kernel,
        out_shape=shapes[0] if single else shapes,
        in_specs=in_specs,
        out_specs=out_spec if single else [out_spec] * len(outs),
        scratch_shapes=scratch,
        compiler_params=pltpu.CompilerParams(vmem_limit_bytes=vmem_mib * 2**20),
        cost_estimate=pl.CostEstimate(flops=flops, bytes_accessed=moved, transcendentals=0),
    )(*args)


def kernel_weights():
    def squares(indices):
        folded = jnp.minimum(indices, NG - indices).astype(F32)
        return folded * folded

    kx = squares(jnp.arange(NG, dtype=jnp.int32))
    ky = squares(lax.axis_index("fft") * SLAB + jnp.arange(SLAB, dtype=jnp.int32))
    kz = squares(jnp.asarray(KZ_FIRST + KZ_REST + KZ_REST, jnp.int32))
    summed = ky[:, None, None] + kx[None, :, None] + kz[None, None, :]
    safe = jnp.maximum(summed, 1.0)
    radius = jnp.sqrt(safe)
    profile = 2.0 * (1.0 - jnp.cos(jnp.pi * radius)) / (jnp.pi * jnp.pi * safe)
    return jnp.where(summed > 0.5, profile, 1.0) * (0.25 / float(NG) ** 1.5)


def shards(wavefunctions, band_occ):
    size = lax.axis_size("band")
    swap = [(g, g ^ 1) for g in range(size)]
    there = [(g, (g - 2 if g % 2 == 0 else g + 2) % size) for g in range(size)]
    back = [(dest, source) for source, dest in there]
    odd = (lax.axis_index("band") % 2).astype(jnp.int32).reshape(1)
    table = {name: jnp.asarray(value) for name, value in tables().items()}
    layout = (STEPS, SENT, LANES)
    payload = ((FFT, BLOCK, LANES), jnp.int16)
    cells = pltpu.VMEM((FFT, PARTS * WINDOW + 56, LANES), F32)
    blocks = pltpu.VMEM((FFT, BLOCK, LANES), F32)
    scales = [pltpu.VMEM((PARTS * FFT, LANES), dtype) for dtype in (F32, jnp.int32)]

    u = call(
        compact_kernel, [(layout, BF16)], [SMEM, VMEM],
        [pltpu.VMEM((ROWS, LANES), F32)], (band_occ, wavefunctions[0]), 0, 4,
    )
    q = lax.ppermute(u, "band", there)
    p = lax.ppermute(u, "band", swap)
    weights = kernel_weights()
    p, weights = lax.optimization_barrier((p, weights))
    sent = call(
        density_kernel, [payload], [SMEM] + [VMEM] * 5 + [ANY],
        [
            pltpu.VMEM((2, 2 * SENT, (STEPS + 2) * LANES), BF16),
            pltpu.VMEM((8, 2 * SENT, 256), F32),
            blocks,
            *scales,
            pltpu.VMEM((2, NG, 256), BF16),
            pltpu.SemaphoreType.DMA,
        ],
        (odd, u, p, q, table["zf"], table["zs"], table["yf"]), 10**9, 20,
    )
    columns = lax.all_to_all(sent, "fft", split_axis=0, concat_axis=0, tiled=True)
    filtered = call(
        filter_kernel, [payload], [VMEM] * 2 + [ANY] * 2,
        [
            cells,
            blocks,
            *scales,
            pltpu.VMEM((2, NG, 256), BF16),
            pltpu.VMEM((2, NG, 256), BF16),
            pltpu.SemaphoreType.DMA((2,)),
        ],
        (columns, weights, table["xf"], table["xb"]), 10**9, 18,
    )
    slabs = lax.all_to_all(filtered, "fft", split_axis=0, concat_axis=0, tiled=True)
    own, to_y, to_z = call(
        product_kernel, [(layout, F32), (layout, jnp.int16), (layout, jnp.int16)],
        [SMEM] + [VMEM] * 6,
        [cells, pltpu.VMEM((8, ROWS + 8, PARTS * LANES), F32), scales[0]],
        (odd, slabs, u, p, q, table["yb"], table["zb"]), 10**9, 24,
    )
    from_z = lax.ppermute(to_z, "band", back)
    from_y = lax.ppermute(to_y, "band", swap)
    result = call(
        sum_kernel, [((SLAB * NG * NG // LANES, 1, LANES), F32)], [VMEM] * 3,
        [pltpu.VMEM((SLAB * NG * NG // LANES, 1, LANES), F32), pltpu.SemaphoreType.DMA((4,))],
        (own, from_y, from_z), 0, 8, ANY,
    )
    return result.reshape(1, SLAB, NG * NG)


def solution(mesh):
    in_specs = (P("band", "fft", None), P("band"))
    out_specs = P("band", "fft", None)
    return jax.shard_map(shards, mesh=mesh, in_specs=in_specs, out_specs=out_specs, check_vma=False)
```

```python
import functools

import jax
import jax.numpy as jnp
import ml_dtypes
import numpy as np
from jax import lax
from jax.experimental import pallas as pl
from jax.experimental.pallas import tpu as pltpu
from jax.sharding import PartitionSpec as P

NG = 176
FFT = 16
SLAB = 11
LANES = 128
STEPS = 11
GROUPS = 22
ROWS = 256
USED = 242
SENT = 248
CELLS = 121
PARTS = 3
BLOCK = 368
WINDOW = 128
PLACES = tuple((part * 120, part * 2) for part in range(PARTS))
F32 = jnp.float32
BF16 = jnp.bfloat16

WINDOWS = []
for _j in range(8):
    _first, _offset = divmod(NG * _j, LANES)
    WINDOWS.append((_first, _offset, -(-(_offset + NG) // LANES)))

SHARED = tuple((first, offset) for first, offset, count in WINDOWS if count == 3)

LOW = list(range(8)) + list(range(168, 176))
KZ_FIRST = list(range(128))
KZ_REST = list(range(128, 176)) + LOW


def split_table(table):
    high = table.astype(ml_dtypes.bfloat16)
    low = (table - high.astype(np.float64)).astype(ml_dtypes.bfloat16)
    return np.stack([high, low])


@functools.cache
def tables():
    index = np.arange(NG)
    phase = (index[:, None] * index[None, :] % NG) * (2.0 * np.pi / NG)
    cas = np.cos(phase) + np.sin(phase)
    lanes = np.array(KZ_FIRST + KZ_REST + KZ_REST)
    z_forward = np.zeros((368, 256))
    z_forward[112 : 112 + NG] = cas[:, lanes]
    z_shared = np.zeros((len(SHARED), 256, 256))
    z_back = np.zeros((8, 256, 256))
    for j, (_first, offset, count) in enumerate(WINDOWS):
        place = offset + np.arange(NG)
        if count == 3:
            place = np.where(place < LANES, place, np.where(place < 256, place, place - 256))
            z_shared[SHARED.index((_first, offset)), place] = cas[:, lanes]
        z_back[j, :128, place] = cas[:, KZ_FIRST]
        z_back[j, 128:192, place] = cas[:, KZ_REST]
    y_forward = np.zeros((NG, 256))
    x_back = np.zeros((NG, 256))
    x_back[:, :NG] = cas
    y_back = np.zeros((FFT, 16, 192))
    x_forward = np.zeros((FFT, 16, NG))
    for j in range(8):
        rows = 8 * np.arange(GROUPS) + j
        y_forward[:, 24 * j : 24 * j + GROUPS] = cas[:, rows]
        y_back[:, :SLAB, 24 * j : 24 * j + GROUPS] = cas[:, rows].reshape(FFT, SLAB, GROUPS)
    x_forward[:, :SLAB] = cas.reshape(FFT, SLAB, NG)
    y_back = y_back.reshape(256, 192).T
    x_forward = x_forward.reshape(256, NG).T
    return {
        "zf": split_table(z_forward),
        "zs": split_table(z_shared),
        "yf": split_table(y_forward),
        "xf": split_table(x_forward),
        "xb": split_table(x_back),
        "yb": split_table(y_back),
        "zb": split_table(z_back),
    }


def halves(value):
    high = value.astype(BF16)
    return high, (value - high.astype(F32)).astype(BF16)


def dot(a, b):
    return jnp.dot(a, b, preferred_element_type=F32)


def dot3(a, b):
    return dot(a[0], b[0]) + dot(a[0], b[1]) + dot(a[1], b[0])


def power_of_two(exponent):
    size = jnp.abs(exponent)
    negative = exponent < 0
    result = jnp.ones(exponent.shape, F32)
    for bit in range(7):
        step = 1 << bit
        factor = jnp.where(negative, F32(2.0**-step), F32(2.0**step))
        result = jnp.where((size & step) != 0, result * factor, result)
    return result


def exponent_of(largest):
    log2 = jnp.log(jnp.maximum(largest, 6.4e-30)) * F32(1.0 / np.log(2.0))
    return (jnp.floor(log2 + 0.001) - 14.0).astype(jnp.int32)


def rounded(value):
    return (value + 12582912.0) - 12582912.0


def largest(*pieces):
    return functools.reduce(
        jnp.maximum, [jnp.max(jnp.abs(piece), axis=0, keepdims=True) for piece in pieces]
    )


def part_pieces(blocks, dest, part):
    window, first = PLACES[part]
    rows = lax.broadcasted_iota(jnp.int32, (8, LANES), 0)
    head = blocks[dest, window : window + 8]
    if first:
        head = jnp.where(rows >= first, head, 0.0)
    tail = jnp.where(rows <= first, blocks[dest, window + 120 : window + 128], 0.0)
    return head, blocks[dest, window + 8 : window + 120], tail


def write_blocks(blocks, out_ref, sizes, exponents, residual_lanes=None):
    for dest in range(FFT):
        for part in range(PARTS):
            row = part * FFT + dest
            sizes[row : row + 1] = largest(*part_pieces(blocks, dest, part))
    exponent = exponent_of(sizes[: PARTS * FFT])
    sizes[: PARTS * FFT] = power_of_two(-exponent)
    if residual_lanes is not None:
        rest = lax.broadcasted_iota(jnp.int32, exponent.shape, 0) >= 2 * FFT
        exponent = jnp.where(rest & residual_lanes, exponent - 15, exponent)
    exponents[: PARTS * FFT] = exponent
    rows = lax.broadcasted_iota(jnp.int32, (8, LANES), 0)
    for dest in range(FFT):
        codes = []
        for part in range(PARTS):
            row = part * FFT + dest
            pieces = []
            for piece in part_pieces(blocks, dest, part):
                scaled = piece * sizes[row : row + 1]
                whole = rounded(scaled)
                if residual_lanes is not None and part == 2:
                    rest = rounded((scaled - whole) * 32768.0)
                    whole = jnp.where(residual_lanes[:1], rest, whole)
                pieces.append(whole.astype(jnp.int32))
            first = PLACES[part][1]
            pieces[2] = jnp.where(rows == first + 1, exponents[row : row + 1], pieces[2])
            if part:
                earlier = codes.pop()
                pieces[0] = jnp.where(rows < first, earlier, pieces[0])
            codes += pieces
        out_ref[dest] = jnp.concatenate(codes, axis=0).astype(jnp.int16)


def read_blocks(in_ref, cells, sizes):
    for source in range(FFT):
        for part, (window, first) in enumerate(PLACES):
            row = part * FFT + source
            tiles = in_ref[source, window + 112 : window + 128].astype(F32)
            sizes[row : row + 1] = tiles[9 + first : 10 + first]
    sizes[: PARTS * FFT] = power_of_two(sizes[: PARTS * FFT].astype(jnp.int32))
    for source in range(FFT):
        block = in_ref[source].astype(jnp.int32)
        for part, (window, _) in enumerate(PLACES):
            row = part * FFT + source
            code = block[window : window + WINDOW].astype(F32)
            cells[source, part * WINDOW : (part + 1) * WINDOW] = code * sizes[row : row + 1]
        cells[source, PARTS * WINDOW :] = jnp.zeros((72, LANES), F32)


def store_field(blocks, lines, field):
    for place, line in enumerate(lines):
        for part in range(PARTS):
            lanes = slice((place * PARTS + part) * LANES, (place * PARTS + part + 1) * LANES)
            start = part * (CELLS + 1) + line * SLAB
            for dest in range(FFT):
                rows = slice(dest * SLAB, (dest + 1) * SLAB)
                blocks[dest, start : start + SLAB] = field[rows, lanes]


def coded(block):
    rows = lax.broadcasted_iota(jnp.int32, (8, LANES), 0)
    pieces = [block[: SENT - 8], jnp.where(rows < 2, block[SENT - 8 :], 0.0)]
    exponent = exponent_of(largest(*pieces))
    scale = power_of_two(-exponent)
    pieces = [rounded(piece * scale).astype(jnp.int32) for piece in pieces]
    pieces[1] = jnp.where(rows == 2, exponent, pieces[1])
    return jnp.concatenate(pieces, axis=0).astype(jnp.int16)


def decoded(block):
    code = block.astype(jnp.int32)
    return code.astype(F32) * power_of_two(code[USED : USED + 1])


def compact_kernel(occ_ref, psi_ref, out_ref, scratch):
    for step in range(STEPS):
        scratch[:ROWS] = jnp.full((ROWS, LANES), occ_ref[0], jnp.int32).astype(F32)
        for group in range(GROUPS):
            tile = (group * STEPS + step) * LANES
            scratch[pl.ds(group, SLAB, stride=GROUPS), :] = psi_ref[:, tile : tile + LANES].astype(F32)
        out_ref[step] = scratch[:SENT].astype(BF16)


def density_kernel(
    odd_ref, u_ref, p_ref, q_ref, zf, zs, yf_ref,
    out_ref, dens, mixed, blocks, sizes, exponents, yf, sem,
):
    copy = pltpu.make_async_copy(yf_ref, yf, sem)
    copy.start()
    odd = odd_ref[0] == 1
    lane = lax.broadcasted_iota(jnp.int32, (2 * SENT, LANES), 1)
    values = {}
    for step in range(STEPS):
        u, p, q = (ref[step].astype(F32) for ref in (u_ref, p_ref, q_ref))
        values[step] = jnp.concatenate([jnp.where(odd, u, q) * p, u * q], axis=0)
        tiles = {step: values[step]}
        for index, (first, offset) in enumerate(SHARED):
            if step == first + 2:
                tiles[STEPS + index] = jnp.where(lane >= offset, values[first], values[step])
        for place, value in tiles.items():
            lanes = slice(place * LANES, (place + 1) * LANES)
            dens[0, :, lanes], dens[1, :, lanes] = halves(value)
    for j, (first, offset, count) in enumerate(WINDOWS):
        if count == 2:
            places = (first, first + 1)
            rows = slice(112 - offset, 368 - offset)
            table = (zf[0, rows], zf[1, rows])
        else:
            index = SHARED.index((first, offset))
            places = (STEPS + index, first + 1)
            table = (zs[0, index], zs[1, index])
        lhs = [
            jnp.concatenate([dens[h, :, k * LANES : (k + 1) * LANES] for k in places], axis=1)
            for h in range(2)
        ]
        mixed[j, : 2 * SENT] = dot3(lhs, table)
    copy.wait()
    low_half = lax.broadcasted_iota(jnp.int32, (192, LANES), 1) < 64

    def plane(x):
        fields = [
            jnp.concatenate(
                [mixed[j, start : start + 24] for j in range(8)], axis=0
            )
            for start in (GROUPS * x, SENT + GROUPS * x)
        ]
        rest = jnp.where(low_half, fields[0][:, LANES:], fields[1][:, LANES:])
        return jnp.concatenate([fields[0][:, :LANES], fields[1][:, :LANES], rest], axis=1)

    for line in range(0, SLAB, 2):
        lines = range(line, min(line + 2, SLAB))
        planes = jnp.concatenate([plane(x) for x in lines], axis=1)
        pad = jnp.zeros((ROWS - 192, planes.shape[1]), BF16)
        field = dot3(
            (yf[0], yf[1]), [jnp.concatenate([half, pad], axis=0) for half in halves(planes)]
        )
        store_field(blocks, lines, field)
    residual = (lax.broadcasted_iota(jnp.int32, (PARTS * FFT, LANES), 1) % 64) >= 48
    write_blocks(blocks, out_ref, sizes, exponents, residual)


def gathered(cells, start):
    parts = []
    for part, (_, first) in enumerate(PLACES):
        begin = part * WINDOW + first + start
        parts.append(
            jnp.concatenate(
                [cells[s, pl.ds(begin, 16, stride=SLAB), :] for s in range(FFT)],
                axis=0,
            )
        )
    return jnp.concatenate(parts, axis=1)


def filter_kernel(
    in_ref, w_ref, xf_ref, xb_ref, out_ref, cells, blocks, sizes, exponents, xf, xb, sems
):
    copies = [
        pltpu.make_async_copy(xf_ref, xf, sems.at[0]),
        pltpu.make_async_copy(xb_ref, xb, sems.at[1]),
    ]
    for copy in copies:
        copy.start()
    read_blocks(in_ref, cells, sizes)
    for copy in copies:
        copy.wait()
    for line in range(0, SLAB, 2):
        lines = range(line, min(line + 2, SLAB))
        columns = jnp.concatenate([gathered(cells, ky) for ky in lines], axis=1)
        spectrum = dot3((xf[0], xf[1]), halves(columns))
        weight = [w_ref[ky] for ky in lines]
        weight = [tile for w in weight for tile in (w[:, :LANES], w)]
        spectrum = spectrum * jnp.concatenate(weight, axis=1)
        pad = jnp.zeros((ROWS - NG, spectrum.shape[1]), BF16)
        field = dot3(
            (xb[0], xb[1]), [jnp.concatenate([half, pad], axis=0) for half in halves(spectrum)]
        )
        store_field(blocks, lines, field)
    write_blocks(blocks, out_ref, sizes, exponents)


def product_kernel(
    odd_ref, in_ref, u_ref, p_ref, q_ref, yb, zb, own_ref, to_y, to_z, cells, mixed, sizes
):
    read_blocks(in_ref, cells, sizes)
    for line in range(0, SLAB, 2):
        lines = range(line, min(line + 2, SLAB))
        columns = jnp.concatenate([gathered(cells, x) for x in lines], axis=1)
        planes = dot3((yb[0], yb[1]), halves(columns))
        for place, x in enumerate(lines):
            lanes = slice(place * PARTS * LANES, (place + 1) * PARTS * LANES)
            for j in range(8):
                mixed[j, GROUPS * x : GROUPS * x + 24] = planes[24 * j : 24 * j + 24, lanes]
    odd = odd_ref[0] == 1

    def occupation(ref):
        return -0.5 * ref[0].astype(F32)[SENT - 1 : SENT]

    f_u, f_p, f_q = occupation(u_ref), occupation(p_ref), occupation(q_ref)
    f_r = jnp.where(odd, f_u, f_q)
    f_own, f_send = jnp.where(odd, f_p, 0.0), jnp.where(odd, 0.0, f_p)

    def finish(step, v1, v2):
        u, p, q = (ref[step].astype(F32) for ref in (u_ref, p_ref, q_ref))
        v1p = v1 * p
        own_ref[step] = f_q * (v2 * q) + f_own * v1p
        to_y[step] = coded(f_r * (v1 * jnp.where(odd, u, q)))
        to_z[step] = coded(f_u * (v2 * u) + f_send * v1p)

    carried = {}
    used = lax.broadcasted_iota(jnp.int32, (SENT, PARTS * LANES), 0) < USED
    lane = lax.broadcasted_iota(jnp.int32, (SENT, LANES), 1)
    for j, (first, offset, count) in enumerate(WINDOWS):
        rows = jnp.where(used, mixed[j, :SENT], 0.0)
        firsts, seconds, rest = (rows[:, part * LANES : (part + 1) * LANES] for part in range(PARTS))
        both = jnp.concatenate(
            [
                jnp.concatenate([firsts, rest], axis=1),
                jnp.concatenate([seconds, pltpu.roll(rest, 64, axis=1)], axis=1),
            ],
            axis=0,
        )
        field = dot3(halves(both), (zb[0, j], zb[1, j]))
        fields = [field[:SENT], field[SENT:]]
        for k in range(count):
            step = first + k
            pieces = [field[:, k % 2 * LANES : (k % 2 + 1) * LANES] for field in fields]
            if count == 3 and k != 1:
                own = lane >= offset if k == 0 else lane < offset
                pieces = [jnp.where(own, piece, 0.0) for piece in pieces]
            if step in carried:
                pieces = [a + b for a, b in zip(carried[step], pieces)]
            carried[step] = pieces
        limit = WINDOWS[j + 1][0] if j < 7 else STEPS
        for step in sorted(carried):
            if step < limit:
                finish(step, *carried.pop(step))


def sum_kernel(own_ref, y_ref, z_ref, out_ref, total, sems):
    scales = [
        [power_of_two(ref[step].astype(jnp.int32)[USED : USED + 1]) for ref in (y_ref, z_ref)]
        for step in range(STEPS)
    ]
    copies = []
    for chunk, start in enumerate(range(0, USED, 64)):
        size = min(64, USED - start)
        for step in range(STEPS):
            value = own_ref[step, start : start + size]
            for ref, scale in zip((y_ref, z_ref), scales[step]):
                value += ref[step, start : start + 64].astype(jnp.int32).astype(F32)[:size] * scale
            total[pl.ds(start * STEPS + step, size, stride=STEPS), 0, :] = value
        rows = pl.ds(start * STEPS, size * STEPS)
        copies.append(pltpu.make_async_copy(total.at[rows], out_ref.at[rows], sems.at[chunk]))
        copies[-1].start()
    for copy in copies:
        copy.wait()


VMEM = pl.BlockSpec(memory_space=pltpu.VMEM)
SMEM = pl.BlockSpec(memory_space=pltpu.SMEM)
ANY = pl.BlockSpec(memory_space=pl.ANY)


def call(kernel, outs, in_specs, scratch, args, flops, vmem_mib, out_spec=VMEM):
    shapes = [jax.ShapeDtypeStruct(*o) for o in outs]
    moved = sum(int(np.prod(a.shape)) * a.dtype.itemsize for a in list(args) + shapes)
    single = len(outs) == 1
    return pl.pallas_call(
        kernel,
        out_shape=shapes[0] if single else shapes,
        in_specs=in_specs,
        out_specs=out_spec if single else [out_spec] * len(outs),
        scratch_shapes=scratch,
        compiler_params=pltpu.CompilerParams(vmem_limit_bytes=vmem_mib * 2**20),
        cost_estimate=pl.CostEstimate(flops=flops, bytes_accessed=moved, transcendentals=0),
    )(*args)


def kernel_weights():
    def squares(indices):
        folded = jnp.minimum(indices, NG - indices).astype(F32)
        return folded * folded

    kx = squares(jnp.arange(NG, dtype=jnp.int32))
    ky = squares(lax.axis_index("fft") * SLAB + jnp.arange(SLAB, dtype=jnp.int32))
    kz = squares(jnp.asarray(KZ_FIRST + KZ_REST + KZ_REST, jnp.int32))
    summed = ky[:, None, None] + kx[None, :, None] + kz[None, None, :]
    safe = jnp.maximum(summed, 1.0)
    radius = jnp.sqrt(safe)
    profile = 2.0 * (1.0 - jnp.cos(jnp.pi * radius)) / (jnp.pi * jnp.pi * safe)
    return jnp.where(summed > 0.5, profile, 1.0) * (0.25 / float(NG) ** 1.5)


def shards(wavefunctions, band_occ):
    size = lax.axis_size("band")
    swap = [(g, g ^ 1) for g in range(size)]
    there = [(g, (g - 2 if g % 2 == 0 else g + 2) % size) for g in range(size)]
    back = [(dest, source) for source, dest in there]
    odd = (lax.axis_index("band") % 2).astype(jnp.int32).reshape(1)
    table = {name: jnp.asarray(value) for name, value in tables().items()}
    layout = (STEPS, SENT, LANES)
    payload = ((FFT, BLOCK, LANES), jnp.int16)
    cells = pltpu.VMEM((FFT, PARTS * WINDOW + 72, LANES), F32)
    blocks = pltpu.VMEM((FFT, BLOCK + 16, LANES), F32)
    scales = [pltpu.VMEM((PARTS * FFT + 16, LANES), dtype) for dtype in (F32, jnp.int32)]

    u = call(
        compact_kernel, [(layout, BF16)], [SMEM, VMEM],
        [pltpu.VMEM((360, LANES), F32)], (band_occ, wavefunctions[0]), 0, 4,
    )
    q = lax.ppermute(u, "band", there)
    p = lax.ppermute(u, "band", swap)
    weights = kernel_weights()
    p, weights = lax.optimization_barrier((p, weights))
    sent = call(
        density_kernel, [payload], [SMEM] + [VMEM] * 5 + [ANY],
        [
            pltpu.VMEM((2, 2 * SENT, (STEPS + 2) * LANES), BF16),
            pltpu.VMEM((8, 2 * SENT + 16, 256), F32),
            blocks,
            *scales,
            pltpu.VMEM((2, NG, 256), BF16),
            pltpu.SemaphoreType.DMA,
        ],
        (odd, u, p, q, table["zf"], table["zs"], table["yf"]), 10**9, 20,
    )
    columns = lax.all_to_all(sent, "fft", split_axis=0, concat_axis=0, tiled=True)
    filtered = call(
        filter_kernel, [payload], [VMEM] * 2 + [ANY] * 2,
        [
            cells,
            blocks,
            *scales,
            pltpu.VMEM((2, NG, 256), BF16),
            pltpu.VMEM((2, NG, 256), BF16),
            pltpu.SemaphoreType.DMA((2,)),
        ],
        (columns, weights, table["xf"], table["xb"]), 10**9, 18,
    )
    slabs = lax.all_to_all(filtered, "fft", split_axis=0, concat_axis=0, tiled=True)
    own, to_y, to_z = call(
        product_kernel, [(layout, F32), (layout, jnp.int16), (layout, jnp.int16)],
        [SMEM] + [VMEM] * 6,
        [cells, pltpu.VMEM((8, ROWS + 16, PARTS * LANES), F32), scales[0]],
        (odd, slabs, u, p, q, table["yb"], table["zb"]), 10**9, 24,
    )
    from_z = lax.ppermute(to_z, "band", back)
    from_y = lax.ppermute(to_y, "band", swap)
    result = call(
        sum_kernel, [((SLAB * NG * NG // LANES, 1, LANES), F32)], [VMEM] * 3,
        [pltpu.VMEM((2736, 1, LANES), F32), pltpu.SemaphoreType.DMA((4,))],
        (own, from_y, from_z), 0, 8, ANY,
    )
    return result.reshape(1, SLAB, NG * NG)


def solution(mesh):
    in_specs = (P("band", "fft", None), P("band"))
    out_specs = P("band", "fft", None)
    return jax.shard_map(shards, mesh=mesh, in_specs=in_specs, out_specs=out_specs, check_vma=False)
```
